32 devices in a mesh: dp: 16 (over z, y, x), band: 2 (over core).
Axes of the slice: x: 2, y: 2, z: 4, core: 2. Of those that a mesh axis runs over, the one named last changes fastest.
Arguments:
- pixels: bfloat16 [32, 254, 896], P('dp', None, 'band'), may hold values from -6 to 6
- time_loc: float32 [32, 8], P(('dp', 'band')), may hold values from -1 to 1
- band_mask: int32 [32, 14], P('dp', 'band'), may hold values from 0 to 1, as said below
- wavelengths: int32 [32, 14], P('dp', 'band'), may hold values from 0 to 15
- visible: int32 [32, 254], P(('dp', 'band')), may hold values from 0 to 1023, as said below
- band_table: bfloat16 [768, 16, 64], P('dp'), may hold values from -1.5 to 1.5
- cls_token: bfloat16 [768], P('dp'), may hold values from -4 to 4
- loc_weight: bfloat16 [768, 8], P('dp'), may hold values from -2 to 2
- enc_attn_gain: bfloat16 [768], P('dp'), may hold values from 0.5 to 1.5
- enc_attn_shift: bfloat16 [768], P('dp'), may hold values from -1 to 1
- enc_qkv: bfloat16 [768, 2304], P('dp'), may hold values from -0.21875 to 0.21875
- enc_out: bfloat16 [768, 768], P('dp'), may hold values from -0.875 to 0.875
- enc_mlp_gain: bfloat16 [768], P('dp'), may hold values from 0.5 to 1.5
- enc_mlp_shift: bfloat16 [768], P('dp'), may hold values from -1 to 1
- enc_up: bfloat16 [768, 3072], P('dp'), may hold values from -0.21875 to 0.21875
- enc_down: bfloat16 [3072, 768], P('dp'), may hold values from -0.109375 to 0.109375
- projection: bfloat16 [768, 512], P('dp'), may hold values from -0.21875 to 0.21875
- mask_token: bfloat16 [512], P('dp'), may hold values from -4 to 4
- dec_attn_gain: bfloat16 [512], P('dp'), may hold values from 0.5 to 1.5
- dec_attn_shift: bfloat16 [512], P('dp'), may hold values from -1 to 1
- dec_qkv: bfloat16 [512, 1536], P('dp'), may hold values from -0.25 to 0.25
- dec_out: bfloat16 [512, 512], P('dp'), may hold values from -1.5 to 1.5
- dec_mlp_gain: bfloat16 [512], P('dp'), may hold values from 0.5 to 1.5
- dec_mlp_shift: bfloat16 [512], P('dp'), may hold values from -1 to 1
- dec_up: bfloat16 [512, 2048], P('dp'), may hold values from -0.25 to 0.25
- dec_down: bfloat16 [2048, 512], P('dp'), may hold values from -0.125 to 0.125
- cotangent: bfloat16 [32, 1024, 512], P(('dp', 'band')), may hold values from -6 to 6
Outputs:
- decoded: bfloat16 [32, 1024, 512], P(('dp', 'band'))
- grad_pixels: float32 [32, 254, 896], P('dp', None, 'band')
- grad_time_loc: float32 [32, 8], P(('dp', 'band'))
- grad_band_table: float32 [768, 16, 64], P('dp')
- grad_cls_token: float32 [768], P('dp')
- grad_loc_weight: float32 [768, 8], P('dp')
- grad_enc_attn_gain: float32 [768], P('dp')
- grad_enc_attn_shift: float32 [768], P('dp')
- grad_enc_qkv: float32 [768, 2304], P('dp')
- grad_enc_out: float32 [768, 768], P('dp')
- grad_enc_mlp_gain: float32 [768], P('dp')
- grad_enc_mlp_shift: float32 [768], P('dp')
- grad_enc_up: float32 [768, 3072], P('dp')
- grad_enc_down: float32 [3072, 768], P('dp')
- grad_projection: float32 [768, 512], P('dp')
- grad_mask_token: float32 [512], P('dp')
- grad_dec_attn_gain: float32 [512], P('dp')
- grad_dec_attn_shift: float32 [512], P('dp')
- grad_dec_qkv: float32 [512, 1536], P('dp')
- grad_dec_out: float32 [512, 512], P('dp')
- grad_dec_mlp_gain: float32 [512], P('dp')
- grad_dec_mlp_shift: float32 [512], P('dp')
- grad_dec_up: float32 [512, 2048], P('dp')
- grad_dec_down: float32 [2048, 512], P('dp')
The draws below stay inside these ranges and needn't reach their ends.
Inputs may be any that keep to these rules, and one draw needn't show every extreme that they name: `band_mask`: band slot 0 of every chip holds a real band. `visible`: the 254 indices of a chip are distinct.
All inputs are finite; a program needn't handle non-finite values.
Results may differ from the reference program's by a relative error of at most 0.03.
Values may be sent and summed in bfloat16 or wider, within the bound.
No kernel may reach another device: no remote copies, remote signals or barrier semaphores. Data moves between devices by JAX's collectives and lax.ppermute only.
A program may use at most 320 MiB of HBM per device.

```python
import math
import jax
import jax.numpy as jnp
from jax import lax

HEADS_ENC = 12
FF_ENC = 3072
HEADS_DEC = 16
FF_DEC = 2048
PATCH_PIX = 64
WAVES = 16
TIMELOC = 8
PATCHES = 1024
D_ENC = 768
D_DEC = 512
BANDS = 14
VIS = 254
CHIPS = 32


def draw_band_mask(key, part):
    draw_bits = jax.random.randint(key, (CHIPS, BANDS), 0, 4)
    live_slots = (draw_bits > 0).astype(jnp.int32)
    first_slot = (jnp.arange(BANDS) == 0).astype(jnp.int32)
    return jnp.maximum(live_slots, first_slot[None, :]).astype(jnp.int32)


def draw_visible(key, part):
    chip_keys = jax.random.split(key, CHIPS)

    def one_chip(chip_key):
        return jax.random.permutation(chip_key, PATCHES)[:VIS]
    return jax.vmap(one_chip)(chip_keys).astype(jnp.int32)


def plant(drawn, rng, smallest, top_value):
    index_at = [jax.random.randint(jax.random.fold_in(rng, axis), (), 0, length) for axis, length in enumerate(drawn.shape)]
    longest = drawn.shape.index(max(drawn.shape))
    next_to = index_at[:longest] + [(index_at[longest] + 1) % drawn.shape[longest]] + index_at[longest + 1:]
    return drawn.at[tuple(index_at)].set(smallest).at[tuple(next_to)].set(top_value)


def shard_levels(stream_key, shape, cuts, least, top_value):
    loudness = 1.0
    for position, parts in cuts:
        steps = jax.random.uniform(jax.random.fold_in(jax.random.fold_in(stream_key, 6), position), (parts,), jnp.float32, least / len(cuts), top_value / len(cuts))
        loudness = loudness * jnp.repeat(jnp.exp(steps), shape[position] // parts).reshape((-1,) + (1,) * (len(shape) - 1 - position))
    return loudness


def noise(rng, extent, scale, most, pieces=(), held_as=jnp.bfloat16):
    drawn = jax.random.normal(rng, extent, jnp.float32) * scale
    if len(pieces) > 0:
        drawn = shard_levels(rng, extent, pieces, -0.22, 0.18) * drawn
    return jnp.clip(drawn, min=-most, max=most).astype(held_as)


def setup_inputs(seed: int = 0) -> dict:
    keys = jax.random.split(jax.random.key(seed), 28)
    return {
        "pixels": noise(keys[0], (CHIPS, VIS, BANDS * PATCH_PIX), 1.0, 6.0, ((0, 16), (2, 2))),
        "time_loc": jnp.clip(jax.random.uniform(keys[1], (CHIPS, TIMELOC), jnp.float32, -1.0, 1.0) * shard_levels(keys[1], (CHIPS, TIMELOC), ((0, 32),), -0.4, 0.0), -1.0, 1.0),
        "band_mask": draw_band_mask(jax.random.fold_in(keys[27], 71), 0),
        "wavelengths": plant(jax.random.randint(keys[3], (CHIPS, BANDS), 0, WAVES), jax.random.fold_in(keys[3], 1), 0, WAVES - 1).astype(jnp.int32),
        "visible": draw_visible(jax.random.fold_in(keys[27], 71), 0),
        "band_table": noise(keys[5], (D_ENC, WAVES, PATCH_PIX), 16 ** -0.5, 1.5, ((0, 16),)),
        "cls_token": noise(keys[6], (D_ENC,), 1.0, 4.0, ((0, 16),)),
        "loc_weight": noise(keys[7], (D_ENC, TIMELOC), TIMELOC ** -0.5, 2.0, ((0, 16),)),
        "enc_attn_gain": jnp.clip(1.0 + 0.1 * jax.random.normal(keys[8], (D_ENC,), jnp.float32), 0.5, 1.5).astype(jnp.bfloat16),
        "enc_attn_shift": noise(keys[9], (D_ENC,), 0.2, 1.0, ((0, 16),)),
        "enc_qkv": noise(keys[10], (D_ENC, 3 * D_ENC), D_ENC ** -0.5, 0.21875, ((0, 16),)),
        "enc_out": noise(keys[11], (D_ENC, D_ENC), (D_ENC // 16) ** -0.5, 0.875, ((0, 16),)),
        "enc_mlp_gain": jnp.clip(1.0 + 0.1 * jax.random.normal(keys[12], (D_ENC,), jnp.float32), 0.5, 1.5).astype(jnp.bfloat16),
        "enc_mlp_shift": noise(keys[13], (D_ENC,), 0.2, 1.0, ((0, 16),)),
        "enc_up": noise(keys[14], (D_ENC, FF_ENC), D_ENC ** -0.5, 0.21875, ((0, 16),)),
        "enc_down": noise(keys[15], (FF_ENC, D_ENC), FF_ENC ** -0.5, 0.109375, ((0, 16),)),
        "projection": noise(keys[16], (D_ENC, D_DEC), D_ENC ** -0.5, 0.21875, ((0, 16),)),
        "mask_token": noise(keys[17], (D_DEC,), 1.0, 4.0, ((0, 16),)),
        "dec_attn_gain": jnp.clip(1.0 + 0.1 * jax.random.normal(keys[18], (D_DEC,), jnp.float32), 0.5, 1.5).astype(jnp.bfloat16),
        "dec_attn_shift": noise(keys[19], (D_DEC,), 0.2, 1.0, ((0, 16),)),
        "dec_qkv": noise(keys[20], (D_DEC, 3 * D_DEC), D_DEC ** -0.5, 0.25, ((0, 16),)),
        "dec_out": noise(keys[21], (D_DEC, D_DEC), (D_DEC // 32) ** -0.5, 1.5, ((0, 16),)),
        "dec_mlp_gain": jnp.clip(1.0 + 0.1 * jax.random.normal(keys[22], (D_DEC,), jnp.float32), 0.5, 1.5).astype(jnp.bfloat16),
        "dec_mlp_shift": noise(keys[23], (D_DEC,), 0.2, 1.0, ((0, 16),)),
        "dec_up": noise(keys[24], (D_DEC, FF_DEC), D_DEC ** -0.5, 0.25, ((0, 16),)),
        "dec_down": noise(keys[25], (FF_DEC, D_DEC), FF_DEC ** -0.5, 0.125, ((0, 16),)),
        "cotangent": noise(keys[26], (CHIPS, PATCHES, D_DEC), 1.0, 6.0, ((0, 32),)),
    }


@jax.custom_vjp
def low(v):
    return lax.optimization_barrier(v.astype(jnp.bfloat16)).astype(jnp.float32)

@jax.custom_vjp
def low_back(v):
    return v

def low_keep(v):
    return (low(v), None)

def low_pass(kept, grad):
    return (grad,)

def back_keep(v):
    return (v, None)

def back_low(kept, grad):
    return (low(grad),)
low.defvjp(low_keep, low_pass)
low_back.defvjp(back_keep, back_low)

def product(left_side, right_side):
    return jnp.dot(left_side, right_side, precision=lax.Precision.HIGHEST)

def sincos(place_index, model_width):
    half_width = model_width // 2
    frequency = jnp.exp(-math.log(10000.0) * jnp.arange(half_width, dtype=jnp.float32) / half_width)
    angles = place_index[..., None] * frequency
    return jnp.concatenate([jnp.sin(angles), jnp.cos(angles)], -1)

def layer_norm(rows_in, gain_row, shift_row):
    centred = rows_in - lax.optimization_barrier(jnp.mean(rows_in, -1, keepdims=True))
    variance = lax.optimization_barrier(jnp.mean(centred * centred, -1, keepdims=True))
    return centred * lax.rsqrt(variance + 1e-05) * gain_row + shift_row

def attention(mixed_rows, head_count):
    length, triple_width = mixed_rows.shape
    model_width = triple_width // 3
    head_size = model_width // head_count
    queries = mixed_rows[:, :model_width].reshape(length, head_count, head_size)
    key_rows = mixed_rows[:, model_width:2 * model_width].reshape(length, head_count, head_size)
    value_rows = mixed_rows[:, 2 * model_width:].reshape(length, head_count, head_size)
    block_rows = min(length, 512)

    def one_block(query_block):
        scores = jnp.einsum('qhe,khe->hqk', query_block, key_rows, precision=lax.Precision.HIGHEST) * head_size ** (-0.5)
        scores = low_back(scores)
        top_score = lax.optimization_barrier(jnp.max(scores, -1, keepdims=True))
        weights = jnp.exp(scores - top_score)
        probability = low(weights / lax.optimization_barrier(jnp.sum(weights, -1, keepdims=True)))
        return jnp.einsum('hqk,khe->qhe', probability, value_rows, precision=lax.Precision.HIGHEST)
    blocks = queries.reshape(length // block_rows, block_rows, head_count, head_size)
    mixed_out = lax.map(jax.checkpoint(one_block), blocks)
    return mixed_out.reshape(length, model_width)

def block_layer(rows_in, weights, head_count):
    gain_one, shift_one, w_qkv, w_out, gain_two, shift_two, w_up, w_down = weights
    normed_one = low(layer_norm(rows_in, gain_one, shift_one))
    mixed_rows = low(low_back(product(normed_one, w_qkv)))
    attn_rows = low(low_back(attention(mixed_rows, head_count)))
    middle = rows_in + low_back(product(attn_rows, w_out))
    normed_two = low(layer_norm(middle, gain_two, shift_two))
    upper = low_back(product(normed_two, w_up))
    active = low(jax.nn.gelu(upper, approximate=True))
    return middle + low_back(product(active, w_down))

def forward_chip(params, pixel_rows, time_row, mask_row, wave_row, visible_row):
    band_table, cls_token, loc_weight = (params[0], params[1], params[2])
    live_slots = mask_row.astype(jnp.float32)
    chosen = jnp.take(band_table, wave_row, axis=1) * live_slots[None, :, None]
    raw_sum = low_back(jnp.einsum('vbp,dbp->vd', pixel_rows, chosen, precision=lax.Precision.HIGHEST))
    patch_rows = raw_sum / jnp.sum(live_slots) + sincos(visible_row.astype(jnp.float32), D_ENC)
    loc_token = product(time_row[None, :], loc_weight.T)
    tokens = jnp.concatenate([cls_token[None, :], loc_token, patch_rows], 0)
    encoded = block_layer(tokens, params[3:11], HEADS_ENC)
    latent = low(low_back(product(low(encoded[2:]), params[11])))
    positions = jnp.arange(PATCHES, dtype=jnp.int32)
    picks = (positions[:, None] == visible_row[None, :]).astype(jnp.float32)
    seen_count = lax.optimization_barrier(jnp.sum(picks, 1, keepdims=True))
    inserted = product(picks, latent) + (1.0 - seen_count) * params[12][None, :] + sincos(positions.astype(jnp.float32), D_DEC)
    return block_layer(inserted, params[13:21], HEADS_DEC)

def reference(pixels, time_loc, band_mask, wavelengths, visible, band_table, cls_token, loc_weight, enc_attn_gain, enc_attn_shift, enc_qkv, enc_out, enc_mlp_gain, enc_mlp_shift, enc_up, enc_down, projection, mask_token, dec_attn_gain, dec_attn_shift, dec_qkv, dec_out, dec_mlp_gain, dec_mlp_shift, dec_up, dec_down, cotangent):
    params = tuple((weight_array.astype(jnp.float32) for weight_array in (band_table, cls_token, loc_weight, enc_attn_gain, enc_attn_shift, enc_qkv, enc_out, enc_mlp_gain, enc_mlp_shift, enc_up, enc_down, projection, mask_token, dec_attn_gain, dec_attn_shift, dec_qkv, dec_out, dec_mlp_gain, dec_mlp_shift, dec_up, dec_down)))

    def chip_step(totals, inputs):
        pixel_rows, time_row, mask_row, wave_row, visible_row, cot_rows = inputs

        def run_chip(weight_set, pixel_float, time_float):
            return forward_chip(weight_set, pixel_float, time_float, mask_row, wave_row, visible_row)
        pixel_float = pixel_rows.astype(jnp.float32).reshape(VIS, BANDS, PATCH_PIX)
        outputs, pull_back = jax.vjp(run_chip, params, pixel_float, time_row.astype(jnp.float32))
        grad_set, grad_pixel, grad_time = pull_back(cot_rows.astype(jnp.float32))
        totals = tuple((first_term + second_term for first_term, second_term in zip(totals, grad_set)))
        return (totals, (outputs.astype(jnp.bfloat16), grad_pixel.reshape(VIS, BANDS * PATCH_PIX), grad_time))
    zeros_start = tuple((jnp.zeros_like(weight_array) for weight_array in params))
    totals, (decoded, grad_pixels, grad_times) = lax.scan(chip_step, zeros_start, (pixels, time_loc, band_mask, wavelengths, visible, cotangent))
    return (decoded, grad_pixels, grad_times, totals[0], totals[1], totals[2], totals[3], totals[4], totals[5], totals[6], totals[7], totals[8], totals[9], totals[10], totals[11], totals[12], totals[13], totals[14], totals[15], totals[16], totals[17], totals[18], totals[19], totals[20])
```

```python
import functools
import math

import jax
import jax.numpy as jnp
from jax import lax
from jax.experimental import pallas as pl
from jax.experimental.pallas import tpu as pltpu
from jax.sharding import PartitionSpec as P

HEADS_ENC = 12
HEADS_DEC = 16
EPSILON = 1e-05
F32 = jnp.float32
BF16 = jnp.bfloat16
BOTH = ("dp", "band")


def dot(a, b, ca, cb):
    return lax.dot_general(a, b, (((ca,), (cb,)), ((), ())), preferred_element_type=F32)


def sincos(place_index, model_width):
    half_width = model_width // 2
    frequency = jnp.exp(-math.log(10000.0) * jnp.arange(half_width, dtype=F32) / half_width)
    angles = place_index[..., None] * frequency
    return jnp.concatenate([jnp.sin(angles), jnp.cos(angles)], -1)


def attend_forward_kernel(q_ref, k_ref, v_ref, out_ref, lse_ref, *, head_size, scale):
    log_scale = scale * math.log2(math.e)
    for first in range(0, q_ref.shape[0], head_size):
        rows = slice(first, first + head_size)
        scores = dot(k_ref[rows], q_ref[rows], 0, 0)
        top = jnp.max(scores, axis=0, keepdims=True) * log_scale
        weights = jnp.exp2(scores * log_scale - top)
        total = jnp.sum(weights, axis=0, keepdims=True)
        mixed = dot(v_ref[rows], weights.astype(BF16), 1, 0)
        out_ref[rows] = (mixed / total).astype(BF16)
        lse_ref[first // head_size] = top + jnp.log2(total)


def attend_forward(mixed_rows, head_count, heads_a_step):
    triple, length = mixed_rows.shape
    width = triple // 3
    head_size = width // head_count
    steps = head_count // heads_a_step
    slab = heads_a_step * head_size
    part = lambda which: pl.BlockSpec((slab, length), lambda h: (which * steps + h, 0))
    return pl.pallas_call(
        functools.partial(attend_forward_kernel, head_size=head_size, scale=head_size**-0.5),
        grid=(steps,),
        in_specs=[part(0), part(1), part(2)],
        out_specs=[part(0), pl.BlockSpec((heads_a_step, 1, length), lambda h: (h, 0, 0))],
        out_shape=[
            jax.ShapeDtypeStruct((width, length), BF16),
            jax.ShapeDtypeStruct((head_count, 1, length), F32),
        ],
        compiler_params=pltpu.CompilerParams(vmem_limit_bytes=40 << 20),
    )(mixed_rows, mixed_rows, mixed_rows)


def attend_backward_kernel(
    q_ref, k_ref, v_ref, out_ref, grad_ref, lse_ref, grad_mixed_ref, *, head_size, scale
):
    log_scale = scale * math.log2(math.e)
    for first in range(0, q_ref.shape[0], head_size):
        rows = slice(first, first + head_size)
        q, k, v, grad = q_ref[rows], k_ref[rows], v_ref[rows], grad_ref[rows]
        delta = jnp.sum(grad.astype(F32) * out_ref[rows].astype(F32), axis=0, keepdims=True)
        probs = jnp.exp2(dot(k, q, 0, 0) * log_scale - lse_ref[first // head_size])
        grad_probs = dot(v, grad, 0, 0)
        grad_scores = (probs * (grad_probs - delta)).astype(BF16)
        grad_mixed_ref[0, rows] = (dot(k, grad_scores, 1, 0) * scale).astype(BF16)
        grad_mixed_ref[1, rows] = (dot(q, grad_scores, 1, 1) * scale).astype(BF16)
        grad_mixed_ref[2, rows] = dot(grad, probs.astype(BF16), 1, 1).astype(BF16)


def attend_backward(mixed_rows, out_rows, grad_rows, lse, head_count, heads_a_step):
    triple, length = mixed_rows.shape
    width = triple // 3
    head_size = width // head_count
    steps = head_count // heads_a_step
    slab = heads_a_step * head_size
    part = lambda which: pl.BlockSpec((slab, length), lambda h: (which * steps + h, 0))
    grads = pl.pallas_call(
        functools.partial(attend_backward_kernel, head_size=head_size, scale=head_size**-0.5),
        grid=(steps,),
        in_specs=[
            part(0),
            part(1),
            part(2),
            part(0),
            part(0),
            pl.BlockSpec((heads_a_step, 1, length), lambda h: (h, 0, 0)),
        ],
        out_specs=pl.BlockSpec((3, slab, length), lambda h: (0, h, 0)),
        out_shape=jax.ShapeDtypeStruct((3, width, length), BF16),
        compiler_params=pltpu.CompilerParams(vmem_limit_bytes=40 << 20),
    )(mixed_rows, mixed_rows, mixed_rows, out_rows, grad_rows, lse)
    return grads.reshape(triple, length)


def norm_forward(rows_in, gain_row, shift_row):
    centred = rows_in - jnp.mean(rows_in, -1, keepdims=True)
    inverse = lax.rsqrt(jnp.mean(centred * centred, -1, keepdims=True) + EPSILON)
    unit_rows = centred * inverse
    return (unit_rows * gain_row + shift_row).astype(BF16), unit_rows, inverse


def norm_backward(grad_normed, unit_rows, inverse, gain_row):
    grad_unit = grad_normed * gain_row
    grad_input = inverse * (
        grad_unit
        - jnp.mean(grad_unit, -1, keepdims=True)
        - unit_rows * jnp.mean(grad_unit * unit_rows, -1, keepdims=True)
    )
    return grad_input, jnp.sum(grad_normed * unit_rows, 0), jnp.sum(grad_normed, 0)


def gelu_tanh(upper):
    return jax.nn.gelu(upper, approximate=True)


def block_forward(rows_in, weights, head_count, heads_a_step):
    gain_one, shift_one, w_qkv, w_out, gain_two, shift_two, w_up, w_down = weights
    normed_one, unit_one, inverse_one = norm_forward(rows_in, gain_one, shift_one)
    mixed_rows = dot(w_qkv, normed_one, 0, 1).astype(BF16)
    attn_rows, lse = attend_forward(mixed_rows, head_count, heads_a_step)
    middle = rows_in + dot(attn_rows, w_out, 0, 0)
    normed_two, unit_two, inverse_two = norm_forward(middle, gain_two, shift_two)
    upper = dot(normed_two, w_up, 1, 0)
    active = gelu_tanh(upper).astype(BF16)
    rows_out = middle + dot(active, w_down, 1, 0)
    saved = (
        unit_one, inverse_one, normed_one, mixed_rows, lse, attn_rows,
        unit_two, inverse_two, normed_two, upper, active,
    )
    return rows_out, saved


def block_backward(grad_out, weights, saved, head_count, heads_a_step):
    gain_one, shift_one, w_qkv, w_out, gain_two, shift_two, w_up, w_down = weights
    (
        unit_one, inverse_one, normed_one, mixed_rows, lse, attn_rows,
        unit_two, inverse_two, normed_two, upper, active,
    ) = saved
    grad_branch = grad_out.astype(BF16)
    grad_down = dot(active, grad_branch, 0, 0).astype(BF16)
    grad_active = dot(grad_branch, w_down, 1, 1)
    grad_upper = jax.vjp(gelu_tanh, upper)[1](grad_active)[0].astype(BF16)
    grad_up = dot(normed_two, grad_upper, 0, 0).astype(BF16)
    grad_normed = dot(grad_upper, w_up, 1, 1)
    grad_middle, grad_gain_two, grad_shift_two = norm_backward(
        grad_normed, unit_two, inverse_two, gain_two
    )
    grad_middle = grad_out + grad_middle
    grad_attn_branch = grad_middle.astype(BF16)
    grad_wout = dot(attn_rows, grad_attn_branch, 1, 0).astype(BF16)
    grad_attn = dot(w_out, grad_attn_branch, 1, 1).astype(BF16)
    grad_mixed = attend_backward(mixed_rows, attn_rows, grad_attn, lse, head_count, heads_a_step)
    grad_qkv = dot(normed_one, grad_mixed, 0, 1).astype(BF16)
    grad_normed_one = dot(grad_mixed, w_qkv, 0, 1)
    grad_input, grad_gain_one, grad_shift_one = norm_backward(
        grad_normed_one, unit_one, inverse_one, gain_one
    )
    vectors = (grad_gain_one, grad_shift_one, grad_gain_two, grad_shift_two)
    return grad_middle + grad_input, vectors, (grad_qkv, grad_wout, grad_up, grad_down)


def swap(array):
    return lax.ppermute(array, "band", [(0, 1), (1, 0)])


def join_pair(mine, axis):
    first = lax.axis_index("band") == 0
    other = swap(mine)
    return jnp.concatenate([jnp.where(first, mine, other), jnp.where(first, other, mine)], axis)


def groups_of(shards):
    rows = 0
    for shard in shards:
        rows = math.gcd(rows, shard.shape[0] // 2)
    return rows


def pack_rows(array, rows):
    lead, (length, width) = array.shape[:-2], array.shape[-2:]
    array = array.reshape(*lead, length // rows, rows, width)
    return jnp.swapaxes(array, -3, -2).reshape(*lead, rows, length // rows * width)


def unpack_rows(array, width):
    lead, (rows, total) = array.shape[:-2], array.shape[-2:]
    array = array.reshape(*lead, rows, total // width, width)
    return jnp.swapaxes(array, -3, -2).reshape(*lead, rows * (total // width), width)


def gather_all(shards):
    rows = groups_of(shards)
    side = lax.axis_index("band")
    halves = [
        lax.dynamic_slice_in_dim(s, side * (s.shape[0] // 2), s.shape[0] // 2, 0) for s in shards
    ]
    packed = jnp.concatenate([pack_rows(h, rows) for h in halves], 1)
    whole = lax.all_gather(packed, BOTH, axis=0, tiled=False)
    out, at = [], 0
    for half in halves:
        span = half.size // rows
        piece = unpack_rows(whole[:, :, at : at + span], half.shape[1])
        out.append(piece.reshape(-1, half.shape[1]))
        at += span
    return out


def scatter_sums(grads, device_count):
    split = [g.reshape(device_count, -1, g.shape[1]) for g in grads]
    rows = 0
    for s in split:
        rows = math.gcd(rows, s.shape[1])
    packed = jnp.concatenate([pack_rows(s, rows) for s in split], 2)
    summed = lax.psum_scatter(packed, BOTH, scatter_dimension=0, tiled=False)
    both = join_pair(summed[None], 0)
    out, at = [], 0
    for s in split:
        span = s.shape[1] * s.shape[2] // rows
        piece = unpack_rows(both[:, :, at : at + span], s.shape[2])
        out.append(piece.reshape(-1, s.shape[2]).astype(F32))
        at += span
    return out


LANES = 128


def columns(vectors):
    stacked = jnp.concatenate([v if v.ndim == 2 else v[:, None] for v in vectors], 1)
    return jnp.pad(stacked, ((0, 0), (0, LANES - stacked.shape[1])))


def per_device(
    pixels, time_loc, band_mask, wavelengths, visible, band_table, cls_token, loc_weight,
    enc_attn_gain, enc_attn_shift, enc_qkv, enc_out, enc_mlp_gain, enc_mlp_shift, enc_up, enc_down,
    projection, mask_token, dec_attn_gain, dec_attn_shift, dec_qkv, dec_out, dec_mlp_gain,
    dec_mlp_shift, dec_up, dec_down, cotangent, *, device_count,
):
    side = lax.axis_index("band")
    table_rows = band_table.shape[0]
    wave_count, pixel_size = band_table.shape[1:]
    (
        table, enc_vectors, w_enc_qkv, w_enc_out, w_enc_up, w_enc_down, w_proj,
        dec_vectors, w_dec_qkv, w_dec_out, w_dec_up, w_dec_down,
    ) = gather_all([
        band_table.reshape(table_rows, -1),
        columns([cls_token, enc_attn_gain, enc_attn_shift, enc_mlp_gain, enc_mlp_shift, loc_weight]),
        enc_qkv, enc_out, enc_up, enc_down, projection,
        columns([mask_token, dec_attn_gain, dec_attn_shift, dec_mlp_gain, dec_mlp_shift]),
        dec_qkv, dec_out, dec_up, dec_down,
    ])
    enc_vec = enc_vectors.T.astype(F32)
    dec_vec = dec_vectors.T.astype(F32)
    loc_rows = enc_vec[5 : 5 + loc_weight.shape[1]]
    enc_weights = (
        enc_vec[1], enc_vec[2], w_enc_qkv, w_enc_out, enc_vec[3], enc_vec[4], w_enc_up, w_enc_down
    )
    dec_weights = (
        dec_vec[1], dec_vec[2], w_dec_qkv, w_dec_out, dec_vec[3], dec_vec[4], w_dec_up, w_dec_down
    )

    def own_chip(array):
        mine = lax.dynamic_index_in_dim(array, side, 0, keepdims=False)
        theirs = lax.dynamic_index_in_dim(array, 1 - side, 0, keepdims=False)
        return jnp.concatenate([mine, swap(theirs)], -1)

    chip_pixels = own_chip(pixels)
    chip_mask = own_chip(band_mask)
    chip_waves = own_chip(wavelengths)
    picks = visible[0]
    slot_wave = (chip_waves[:, None] == jnp.arange(wave_count, dtype=jnp.int32)) & (
        chip_mask[:, None] > 0
    )
    same_pixel = jnp.arange(pixel_size)[:, None] == jnp.arange(pixel_size)
    spread = (slot_wave[:, None, :, None] & same_pixel[None, :, None, :]).astype(BF16)
    spread = spread.reshape(chip_pixels.shape[1], wave_count * pixel_size)
    wave_pixels = dot(chip_pixels, spread, 1, 0).astype(BF16)
    band_count = jnp.sum(chip_mask).astype(F32)

    width = table.shape[0]
    patch_rows = dot(wave_pixels, table, 1, 1) / band_count + sincos(picks.astype(F32), width)
    loc_token = jnp.dot(time_loc, loc_rows, precision=lax.Precision.HIGHEST)
    tokens = jnp.concatenate([enc_vec[0:1], loc_token, patch_rows], 0)
    encoded, enc_saved = block_forward(tokens, enc_weights, HEADS_ENC, HEADS_ENC)
    latent_in = encoded[2:].astype(BF16)
    latent = dot(latent_in, w_proj, 1, 0).astype(BF16)

    positions = jnp.arange(cotangent.shape[1], dtype=jnp.int32)
    matches = positions[:, None] == picks[None, :]
    hidden = 1.0 - jnp.sum(matches.astype(F32), 1, keepdims=True)
    matches = matches.astype(BF16)
    inserted = (
        dot(matches, latent, 1, 0)
        + hidden * dec_vec[0]
        + sincos(positions.astype(F32), latent.shape[1])
    )
    decoded, dec_saved = block_forward(inserted, dec_weights, HEADS_DEC, 1)
    grad_inserted, dec_vec_grads, dec_grads = block_backward(
        cotangent[0].astype(F32), dec_weights, dec_saved, HEADS_DEC, 1
    )
    grad_mask = jnp.sum(grad_inserted * hidden, 0)
    grad_latent = dot(matches, grad_inserted.astype(BF16), 0, 0).astype(BF16)
    grad_proj = dot(latent_in, grad_latent, 0, 0).astype(BF16)
    grad_rows = dot(grad_latent, w_proj, 1, 1)
    dec_sums = scatter_sums(
        [grad_proj, columns((grad_mask,) + dec_vec_grads).astype(BF16), *dec_grads], device_count
    )

    grad_encoded = jnp.concatenate([jnp.zeros((2, width), F32), grad_rows], 0)
    grad_tokens, enc_vec_grads, enc_grads = block_backward(
        grad_encoded, enc_weights, enc_saved, HEADS_ENC, HEADS_ENC
    )
    grad_loc_row = grad_tokens[1:2]
    grad_loc = jnp.dot(grad_loc_row.T, time_loc, precision=lax.Precision.HIGHEST)
    grad_time = jnp.dot(grad_loc_row, loc_rows.T, precision=lax.Precision.HIGHEST)
    grad_raw = (grad_tokens[2:] / band_count).astype(BF16)
    grad_table = dot(grad_raw, wave_pixels, 0, 0).astype(BF16)
    grad_waves = dot(grad_raw, table, 1, 0).astype(BF16)
    grad_chip = dot(grad_waves, spread, 1, 1).astype(BF16)
    here = grad_chip.shape[1] // 2
    mine, theirs = grad_chip[:, :here], swap(grad_chip[:, here:])
    grad_pixels = jnp.where(
        side == 0, jnp.stack([mine, theirs]), jnp.stack([theirs, mine])
    ).astype(F32)
    enc_sums = scatter_sums(
        [
            grad_table,
            columns((grad_tokens[0],) + enc_vec_grads + (grad_loc,)).astype(BF16),
            *enc_grads,
        ],
        device_count,
    )
    s_table, s_enc_vec, s_enc_qkv, s_enc_out, s_enc_up, s_enc_down = enc_sums
    s_proj, s_dec_vec, s_dec_qkv, s_dec_out, s_dec_up, s_dec_down = dec_sums
    return (
        decoded.astype(BF16)[None],
        grad_pixels,
        grad_time,
        s_table.reshape(band_table.shape),
        s_enc_vec[:, 0],
        s_enc_vec[:, 5 : 5 + loc_weight.shape[1]],
        s_enc_vec[:, 1],
        s_enc_vec[:, 2],
        s_enc_qkv,
        s_enc_out,
        s_enc_vec[:, 3],
        s_enc_vec[:, 4],
        s_enc_up,
        s_enc_down,
        s_proj,
        s_dec_vec[:, 0],
        s_dec_vec[:, 1],
        s_dec_vec[:, 2],
        s_dec_qkv,
        s_dec_out,
        s_dec_vec[:, 3],
        s_dec_vec[:, 4],
        s_dec_up,
        s_dec_down,
    )


def solution(mesh):
    dp, chip, both, matrix = P("dp"), P("dp", "band"), P(BOTH, None), P("dp", None)
    block = (dp, dp, matrix, matrix, dp, dp, matrix, matrix)
    in_specs = (
        P("dp", None, "band"), both, chip, chip, both,
        P("dp", None, None), dp, matrix, *block, matrix, dp, *block, P(BOTH, None, None),
    )
    out_specs = (
        P(BOTH, None, None), P("dp", None, "band"), both,
        P("dp", None, None), dp, matrix, *block, matrix, dp, *block,
    )
    return jax.shard_map(
        functools.partial(per_device, device_count=mesh.size),
        mesh=mesh, in_specs=in_specs, out_specs=out_specs, check_vma=False,
    )
```

```python
import functools
import math

import jax
import jax.numpy as jnp
from jax import lax
from jax.experimental import pallas as pl
from jax.experimental.pallas import tpu as pltpu
from jax.sharding import PartitionSpec as P

HEADS_ENC = 12
HEADS_DEC = 16
EPSILON = 1e-05
F32 = jnp.float32
BF16 = jnp.bfloat16
BOTH = ("dp", "band")


def dot(a, b, ca, cb):
    return lax.dot_general(a, b, (((ca,), (cb,)), ((), ())), preferred_element_type=F32)


def sincos(place_index, model_width):
    half_width = model_width // 2
    frequency = jnp.exp(-math.log(10000.0) * jnp.arange(half_width, dtype=F32) / half_width)
    angles = place_index[..., None] * frequency
    return jnp.concatenate([jnp.sin(angles), jnp.cos(angles)], -1)


def attend_forward_kernel(q_ref, k_ref, v_ref, out_ref, lse_ref, *, head_size, scale):
    log_scale = scale * math.log2(math.e)
    for first in range(0, q_ref.shape[0], head_size):
        rows = slice(first, first + head_size)
        scores = dot(k_ref[rows], q_ref[rows], 0, 0)
        top = jnp.max(scores, axis=0, keepdims=True) * log_scale
        weights = jnp.exp2(scores * log_scale - top)
        total = jnp.sum(weights, axis=0, keepdims=True)
        mixed = dot(v_ref[rows], weights.astype(BF16), 1, 0)
        out_ref[rows] = (mixed / total).astype(BF16)
        lse_ref[first // head_size] = top + jnp.log2(total)


def attend_forward(mixed_rows, head_count, heads_a_step):
    triple, length = mixed_rows.shape
    width = triple // 3
    head_size = width // head_count
    steps = head_count // heads_a_step
    slab = heads_a_step * head_size
    part = lambda which: pl.BlockSpec((slab, length), lambda h: (which * steps + h, 0))
    return pl.pallas_call(
        functools.partial(attend_forward_kernel, head_size=head_size, scale=head_size**-0.5),
        grid=(steps,),
        in_specs=[part(0), part(1), part(2)],
        out_specs=[part(0), pl.BlockSpec((heads_a_step, 1, length), lambda h: (h, 0, 0))],
        out_shape=[
            jax.ShapeDtypeStruct((width, length), BF16),
            jax.ShapeDtypeStruct((head_count, 1, length), F32),
        ],
        compiler_params=pltpu.CompilerParams(vmem_limit_bytes=40 << 20),
    )(mixed_rows, mixed_rows, mixed_rows)


def attend_backward_kernel(
    q_ref, k_ref, v_ref, out_ref, grad_ref, lse_ref, *rest, head_size, scale
):
    grad_mixed_ref = rest[-1]
    log_scale = scale * math.log2(math.e)
    for first in range(0, q_ref.shape[0], head_size):
        rows = slice(first, first + head_size)
        q, k, v, grad = q_ref[rows], k_ref[rows], v_ref[rows], grad_ref[rows]
        delta = jnp.sum(grad.astype(F32) * out_ref[rows].astype(F32), axis=0, keepdims=True)
        probs = jnp.exp2(dot(k, q, 0, 0) * log_scale - lse_ref[first // head_size])
        grad_probs = dot(v, grad, 0, 0)
        grad_scores = (probs * (grad_probs - delta)).astype(BF16)
        grad_mixed_ref[0, rows] = (dot(k, grad_scores, 1, 0) * scale).astype(BF16)
        grad_mixed_ref[1, rows] = (dot(q, grad_scores, 1, 1) * scale).astype(BF16)
        grad_mixed_ref[2, rows] = dot(grad, probs.astype(BF16), 1, 1).astype(BF16)


def attend_backward(
    mixed_rows, out_rows, grad_rows, lse, head_count, heads_a_step, share=(0, 1), before=None
):
    triple, length = mixed_rows.shape
    width = triple // 3
    head_size = width // head_count
    total = head_count // heads_a_step
    steps = total // share[1]
    start = share[0] * steps
    slab = heads_a_step * head_size
    part = lambda which: pl.BlockSpec((slab, length), lambda h: (which * total + start + h, 0))
    extra = [] if before is None else [before]
    return pl.pallas_call(
        functools.partial(attend_backward_kernel, head_size=head_size, scale=head_size**-0.5),
        grid=(steps,),
        in_specs=[
            part(0),
            part(1),
            part(2),
            part(0),
            part(0),
            pl.BlockSpec((heads_a_step, 1, length), lambda h: (start + h, 0, 0)),
        ]
        + [pl.BlockSpec(memory_space=pl.ANY) for _ in extra],
        out_specs=pl.BlockSpec((3, slab, length), lambda h: (0, start + h, 0)),
        out_shape=jax.ShapeDtypeStruct((3, width, length), BF16),
        input_output_aliases={6: 0} if extra else {},
        compiler_params=pltpu.CompilerParams(vmem_limit_bytes=40 << 20),
    )(mixed_rows, mixed_rows, mixed_rows, out_rows, grad_rows, lse, *extra)


def norm_forward(rows_in, gain_row, shift_row):
    centred = rows_in - jnp.mean(rows_in, -1, keepdims=True)
    inverse = lax.rsqrt(jnp.mean(centred * centred, -1, keepdims=True) + EPSILON)
    unit_rows = centred * inverse
    return (unit_rows * gain_row + shift_row).astype(BF16), unit_rows, inverse


def norm_backward(grad_normed, unit_rows, inverse, gain_row):
    grad_unit = grad_normed * gain_row
    grad_input = inverse * (
        grad_unit
        - jnp.mean(grad_unit, -1, keepdims=True)
        - unit_rows * jnp.mean(grad_unit * unit_rows, -1, keepdims=True)
    )
    return grad_input, jnp.sum(grad_normed * unit_rows, 0), jnp.sum(grad_normed, 0)


def gelu_tanh(upper):
    return jax.nn.gelu(upper, approximate=True)


def block_forward(rows_in, weights, head_count, heads_a_step):
    gain_one, shift_one, w_qkv, w_out, gain_two, shift_two, w_up, w_down = weights
    normed_one, unit_one, inverse_one = norm_forward(rows_in, gain_one, shift_one)
    mixed_rows = dot(w_qkv, normed_one, 0, 1).astype(BF16)
    attn_rows, lse = attend_forward(mixed_rows, head_count, heads_a_step)
    middle = rows_in + dot(attn_rows, w_out, 0, 0)
    normed_two, unit_two, inverse_two = norm_forward(middle, gain_two, shift_two)
    upper = dot(normed_two, w_up, 1, 0)
    active = gelu_tanh(upper).astype(BF16)
    rows_out = middle + dot(active, w_down, 1, 0)
    saved = (
        unit_one, inverse_one, normed_one, mixed_rows, lse, attn_rows,
        unit_two, inverse_two, normed_two, upper, active,
    )
    return rows_out, saved


def mlp_backward(grad_out, weights, saved):
    gain_two, w_out, w_up, w_down = weights[4], weights[3], weights[6], weights[7]
    unit_two, inverse_two, upper = saved[6], saved[7], saved[9]
    grad_branch = grad_out.astype(BF16)
    grad_active = dot(grad_branch, w_down, 1, 1)
    grad_upper = jax.vjp(gelu_tanh, upper)[1](grad_active)[0].astype(BF16)

    def rest(grad_upper):
        grad_normed = dot(grad_upper, w_up, 1, 1)
        grad_middle, grad_gain_two, grad_shift_two = norm_backward(
            grad_normed, unit_two, inverse_two, gain_two
        )
        grad_middle = grad_out + grad_middle
        grad_attn_branch = grad_middle.astype(BF16)
        grad_attn = dot(w_out, grad_attn_branch, 1, 1).astype(BF16)
        return grad_middle, grad_attn_branch, grad_attn, (grad_gain_two, grad_shift_two)

    return grad_branch, grad_upper, rest


def attn_backward(grad_attn, saved, head_count, heads_a_step, share=(0, 1), before=None):
    return attend_backward(
        saved[3], saved[5], grad_attn, saved[4], head_count, heads_a_step, share, before
    )


def input_backward(grad_middle, grad_mixed, weights, saved):
    grad_normed_one = dot(grad_mixed, weights[2], 0, 1)
    grad_input, grad_gain_one, grad_shift_one = norm_backward(
        grad_normed_one, saved[0], saved[1], weights[0]
    )
    return grad_middle + grad_input, (grad_gain_one, grad_shift_one)


def swap(array):
    return lax.ppermute(array, "band", [(0, 1), (1, 0)])


def join_pair(mine, axis):
    first = lax.axis_index("band") == 0
    other = swap(mine)
    return jnp.concatenate([jnp.where(first, mine, other), jnp.where(first, other, mine)], axis)


def groups_of(shards):
    rows = 0
    for shard in shards:
        rows = math.gcd(rows, shard.shape[0] // 2)
    return rows


def pack_rows(array, rows):
    lead, (length, width) = array.shape[:-2], array.shape[-2:]
    array = array.reshape(*lead, length // rows, rows, width)
    return jnp.swapaxes(array, -3, -2).reshape(*lead, rows, length // rows * width)


def unpack_rows(array, width):
    lead, (rows, total) = array.shape[:-2], array.shape[-2:]
    array = array.reshape(*lead, rows, total // width, width)
    return jnp.swapaxes(array, -3, -2).reshape(*lead, rows * (total // width), width)


def gather_all(shards):
    rows = groups_of(shards)
    side = lax.axis_index("band")
    halves = [
        lax.dynamic_slice_in_dim(s, side * (s.shape[0] // 2), s.shape[0] // 2, 0) for s in shards
    ]
    packed = jnp.concatenate([pack_rows(h, rows) for h in halves], 1)
    whole = lax.all_gather(packed, BOTH, axis=0, tiled=False)
    out, at = [], 0
    for half in halves:
        span = half.size // rows
        piece = unpack_rows(whole[:, :, at : at + span], half.shape[1])
        out.append(piece.reshape(-1, half.shape[1]))
        at += span
    return out


def pack_grads(grads, device_count):
    split = [g.reshape(device_count, -1, g.shape[1]) for g in grads]
    rows = 0
    for s in split:
        rows = math.gcd(rows, s.shape[1])
    return jnp.concatenate([pack_rows(s, rows) for s in split], 2)


def unpack_sums(summed, shapes):
    both = join_pair(summed[None], 0)
    rows = both.shape[1]
    out, at = [], 0
    for length, width in shapes:
        span = length // 2 * width // rows
        piece = unpack_rows(both[:, :, at : at + span], width)
        out.append(piece.reshape(length, width).astype(F32))
        at += span
    return out


def scatter_sums(grads, device_count):
    packed = pack_grads(grads, device_count)
    summed = lax.psum_scatter(packed, BOTH, scatter_dimension=0, tiled=False)
    dp_count = device_count // 2
    return unpack_sums(summed, [(g.shape[0] // dp_count, g.shape[1]) for g in grads])


LANES = 128
TILE = 16


def columns(vectors, lanes=LANES):
    stacked = jnp.concatenate([v if v.ndim == 2 else v[:, None] for v in vectors], 1)
    return jnp.pad(stacked, ((0, 0), (0, lanes - stacked.shape[1])))


def hop(flips):
    return [
        (dp * 2 + band, (dp ^ flips[band]) * 2 + band) for dp in range(16) for band in range(2)
    ]


FIRST_HOP = hop((2, 1))
SECOND_HOP = hop((1, 2))


def places(shapes):
    out, at = [], 0
    for rows, half in shapes:
        out.append((rows, half, at))
        at += rows // TILE * half
    return out, at


def lay(dst, src, rows, half, at):
    for group in range(rows // TILE):
        dst[:, at + group * half : at + (group + 1) * half] = src[group * TILE : (group + 1) * TILE]


def products_of(jobs, spots, refs, which):
    ins = list(refs)
    for (left_axis, right_axis), spot in zip(jobs, spots):
        left = None if left_axis is None else ins.pop(0)
        right = ins.pop(0)
        half = spot[1]
        span = pl.ds(pl.multiple_of(which * half, 128), half)
        values = right[span] if right_axis == 1 else right[:, span]
        yield values if left is None else dot(left[...], values, left_axis, right_axis)


def send_kernel(scalars, *refs, jobs, spots):
    out = refs[-1]
    halves = products_of(jobs, spots, refs[:-1], 1 - scalars[0])
    for values, (rows, half, at) in zip(halves, spots):
        values = values.astype(BF16)
        for block in range(16):
            lay(out.at[block], values[block * rows : (block + 1) * rows], rows, half, at)


def keep_kernel(scalars, *refs, jobs, spots):
    count = len(spots)
    arrived, send, keep, landed, sem = refs[-count - 5 : -count]
    copy = pltpu.make_async_copy(arrived, landed, sem)
    copy.start()
    halves = products_of(jobs, spots, refs[: -count - 5], scalars[0])
    for values, held in zip(halves, refs[-count:]):
        held[...] = values.astype(F32)
    copy.wait()
    for held, (rows, half, at) in zip(refs[-count:], spots):
        for step in range(16):
            block = scalars[1 + step]
            out = (send if step < 8 else keep).at[step % 8]
            for group in range(rows // TILE):
                span = slice(at + group * half, at + (group + 1) * half)
                own = held[pl.ds(pl.multiple_of(block * rows + group * TILE, TILE), TILE)]
                out[:, span] = (own + landed[block, :, span].astype(F32)).astype(BF16)


def split_kernel(table, own_send, own_keep, recv_send, recv_keep, send, keep):
    send[...] = (own_send[...].astype(F32) + recv_send[...].astype(F32)).astype(BF16)
    keep[...] = (own_keep[...].astype(F32) + recv_keep[...].astype(F32)).astype(BF16)


def unpack_kernel(scalars, mine, theirs, *outs, spots):
    side = scalars[0]
    for source, which in ((mine, side), (theirs, 1 - side)):
        for out, (rows, half, at) in zip(outs, spots):
            for group in range(rows // TILE):
                span = slice(at + group * half, at + (group + 1) * half)
                lanes = pl.ds(pl.multiple_of(which * half, 128), half)
                out[group * TILE : (group + 1) * TILE, lanes] = source[:, span].astype(F32)


def grid_call(kernel, scalars, grid, in_specs, out_specs, out_shape, *args):
    return pl.pallas_call(
        kernel,
        grid_spec=pltpu.PrefetchScalarGridSpec(
            num_scalar_prefetch=1, grid=grid, in_specs=in_specs, out_specs=out_specs
        ),
        out_shape=out_shape,
        compiler_params=pltpu.CompilerParams(vmem_limit_bytes=40 << 20),
    )(scalars, *args)


def vmem_call(kernel, out_shape, *args, away=0, scratch_shapes=()):
    whole = pl.BlockSpec(memory_space=pltpu.VMEM)
    return pl.pallas_call(
        kernel,
        in_specs=[pl.BlockSpec(memory_space=pltpu.SMEM)]
        + [whole] * (len(args) - 1 - away)
        + [pl.BlockSpec(memory_space=pl.ANY)] * away,
        out_specs=[whole] * len(out_shape),
        out_shape=out_shape,
        scratch_shapes=scratch_shapes,
        compiler_params=pltpu.CompilerParams(vmem_limit_bytes=56 << 20),
    )(*args)


class Bucket:
    def __init__(self, products):
        dp, side = lax.axis_index("dp"), lax.axis_index("band")
        self.x, self.y, self.z, self.side = dp % 2, dp // 2 % 2, dp // 4, side
        self.scalars = side[None].astype(jnp.int32)
        shapes, self.jobs, self.args = [], [], []
        for left, left_axis, right, right_axis in products:
            length = right.shape[0] if left is None else left.shape[1 - left_axis]
            shapes.append((length // 16, right.shape[1 - right_axis] // 2))
            self.jobs.append((left_axis, right_axis))
            self.args += [right] if left is None else [left, right]
        self.spots, self.total = places(shapes)
        (self.send,) = vmem_call(
            functools.partial(send_kernel, jobs=self.jobs, spots=self.spots),
            [self.shaped(16)],
            self.scalars,
            *self.args,
        )

    def shaped(self, count):
        return jax.ShapeDtypeStruct((count, TILE, self.total), BF16)

    def block(self, index):
        return pl.BlockSpec((1, TILE, self.total), index)

    def split(self, count, table, goes, stays):
        goes, stays, out = self.block(goes), self.block(stays), self.block(lambda i, t: (i, 0, 0))
        self.send, self.keep = grid_call(
            split_kernel,
            table.astype(jnp.int32),
            (count,),
            [goes, stays, goes, stays],
            [out] * 2,
            [self.shaped(count)] * 2,
            self.keep,
            self.keep,
            self.arrived,
            self.arrived,
        )

    def pair_hop(self):
        self.arrived = swap(self.send)

    def first_hop(self, clock):
        self.arrived, clock = tie(self.arrived, clock)
        line = jnp.arange(8, dtype=jnp.int32)
        z, other = line // 2, line % 2
        near = jnp.where(self.side == 0, self.y, self.x)
        place = lambda bit: z * 4 + jnp.where(self.side == 0, bit * 2 + other, other * 2 + bit)
        table = jnp.concatenate([self.side[None], place(1 - near), place(near)])
        self.send, self.keep = vmem_call(
            functools.partial(keep_kernel, jobs=self.jobs, spots=self.spots),
            [self.shaped(8)] * 2,
            table.astype(jnp.int32),
            *self.args,
            self.arrived,
            away=1,
            scratch_shapes=[pltpu.VMEM((16, TILE, self.total), BF16), pltpu.SemaphoreType.DMA(())]
            + [pltpu.VMEM((16 * rows, half), F32) for rows, half, _ in self.spots],
        )
        self.arrived = lax.ppermute(self.send, BOTH, FIRST_HOP)
        return self.send

    def later_hop(self, clock, count, bit, pairs):
        self.arrived, clock = tie(self.arrived, clock)
        self.split(
            count,
            bit[None],
            lambda i, t: (2 * i + 1 - t[0], 0, 0),
            lambda i, t: (2 * i + t[0], 0, 0),
        )
        self.arrived = lax.ppermute(self.send, BOTH, pairs)
        return self.send

    def second_hop(self, clock):
        far = jnp.where(self.side == 0, self.x, self.y)
        return self.later_hop(clock, 4, far, SECOND_HOP)

    def third_hop(self, clock):
        return self.later_hop(clock, 2, self.z % 2, hop((4, 4)))

    def fourth_hop(self, clock):
        return self.later_hop(clock, 1, self.z // 2, hop((8, 8)))

    def finish(self):
        mine = (self.keep[0].astype(F32) + self.arrived[0].astype(F32)).astype(BF16)
        return vmem_call(
            functools.partial(unpack_kernel, spots=self.spots),
            [jax.ShapeDtypeStruct((r, 2 * h), F32) for r, h, _ in self.spots],
            self.scalars,
            mine,
            swap(mine),
        )


def tie(first, second):
    return lax.optimization_barrier((first, second))


def per_device(
    pixels, time_loc, band_mask, wavelengths, visible, band_table, cls_token, loc_weight,
    enc_attn_gain, enc_attn_shift, enc_qkv, enc_out, enc_mlp_gain, enc_mlp_shift, enc_up, enc_down,
    projection, mask_token, dec_attn_gain, dec_attn_shift, dec_qkv, dec_out, dec_mlp_gain,
    dec_mlp_shift, dec_up, dec_down, cotangent, *, device_count,
):
    side = lax.axis_index("band")
    table_rows = band_table.shape[0]
    wave_count, pixel_size = band_table.shape[1:]
    (
        table, enc_vectors, w_enc_qkv, w_enc_out, w_enc_up, w_enc_down, w_proj,
        dec_vectors, w_dec_qkv, w_dec_out, w_dec_up, w_dec_down,
    ) = gather_all([
        band_table.reshape(table_rows, -1),
        columns([cls_token, enc_attn_gain, enc_attn_shift, enc_mlp_gain, enc_mlp_shift, loc_weight]),
        enc_qkv, enc_out, enc_up, enc_down, projection,
        columns([mask_token, dec_attn_gain, dec_attn_shift, dec_mlp_gain, dec_mlp_shift]),
        dec_qkv, dec_out, dec_up, dec_down,
    ])
    enc_vec = enc_vectors.T.astype(F32)
    dec_vec = dec_vectors.T.astype(F32)
    loc_rows = enc_vec[5 : 5 + loc_weight.shape[1]]
    enc_weights = (
        enc_vec[1], enc_vec[2], w_enc_qkv, w_enc_out, enc_vec[3], enc_vec[4], w_enc_up, w_enc_down
    )
    dec_weights = (
        dec_vec[1], dec_vec[2], w_dec_qkv, w_dec_out, dec_vec[3], dec_vec[4], w_dec_up, w_dec_down
    )

    def own_chip(array):
        mine = lax.dynamic_index_in_dim(array, side, 0, keepdims=False)
        theirs = lax.dynamic_index_in_dim(array, 1 - side, 0, keepdims=False)
        return jnp.concatenate([mine, swap(theirs)], -1)

    chip_pixels = own_chip(pixels)
    chip_mask = own_chip(band_mask)
    chip_waves = own_chip(wavelengths)
    picks = visible[0]
    slot_wave = (chip_waves[:, None] == jnp.arange(wave_count, dtype=jnp.int32)) & (
        chip_mask[:, None] > 0
    )
    same_pixel = jnp.arange(pixel_size)[:, None] == jnp.arange(pixel_size)
    spread = (slot_wave[:, None, :, None] & same_pixel[None, :, None, :]).astype(BF16)
    spread = spread.reshape(chip_pixels.shape[1], wave_count * pixel_size)
    wave_pixels = jnp.pad(dot(chip_pixels, spread, 1, 0).astype(BF16), ((2, 0), (0, 0)))
    picks = jnp.pad(picks, (2, 0), constant_values=-1)
    band_count = jnp.sum(chip_mask).astype(F32)

    width = table.shape[0]
    patch_rows = dot(wave_pixels, table, 1, 1) / band_count + sincos(picks.astype(F32), width)
    loc_token = jnp.dot(time_loc, loc_rows, precision=lax.Precision.HIGHEST)
    tokens = jnp.concatenate([enc_vec[0:1], loc_token, patch_rows[2:]], 0)
    encoded, enc_saved = block_forward(tokens, enc_weights, HEADS_ENC, HEADS_ENC)
    latent_in = encoded.astype(BF16)
    latent = dot(latent_in, w_proj, 1, 0).astype(BF16)

    positions = jnp.arange(cotangent.shape[1], dtype=jnp.int32)
    matches = positions[:, None] == picks[None, :]
    hidden = 1.0 - jnp.sum(matches.astype(F32), 1, keepdims=True)
    matches = matches.astype(BF16)
    inserted = (
        dot(matches, latent, 1, 0)
        + hidden * dec_vec[0]
        + sincos(positions.astype(F32), latent.shape[1])
    )
    decoded, dec_saved = block_forward(inserted, dec_weights, HEADS_DEC, 1)
    fast = device_count == 32
    grad_out = cotangent[0].astype(F32)
    dec_branch, dec_upper, rest = mlp_backward(grad_out, dec_weights, dec_saved)
    grad_middle, dec_attn_branch, grad_attn, dec_norm_two = rest(dec_upper)
    dec_products = (
        (dec_saved[10], 0, dec_branch, 0),
        (dec_saved[8], 0, dec_upper, 0),
        (dec_saved[5], 1, dec_attn_branch, 0),
    )
    if fast:
        early = Bucket(dec_products)
        grad_attn, early.send = tie(grad_attn, early.send)
        early.pair_hop()
        dec_mixed = attn_backward(grad_attn, dec_saved, HEADS_DEC, 1, (0, 2))
        dec_mixed, early.send = tie(dec_mixed, early.first_hop(dec_mixed))
        dec_mixed = attn_backward(grad_attn, dec_saved, HEADS_DEC, 1, (1, 2), dec_mixed)
        dec_mixed, early.send = tie(dec_mixed, early.second_hop(dec_mixed))
    else:
        dec_mixed = attn_backward(grad_attn, dec_saved, HEADS_DEC, 1)
    dec_mixed = dec_mixed.reshape(dec_saved[3].shape)
    grad_inserted, dec_norm_one = input_backward(grad_middle, dec_mixed, dec_weights, dec_saved)
    grad_mask = jnp.sum(grad_inserted * hidden, 0)
    dec_vec_grads = columns((grad_mask, *dec_norm_one, *dec_norm_two), 2 * LANES).astype(BF16)
    grad_latent = dot(matches, grad_inserted.astype(BF16), 0, 0).astype(BF16)
    grad_encoded = dot(grad_latent, w_proj, 1, 1)

    enc_branch, enc_upper, rest = mlp_backward(grad_encoded, enc_weights, enc_saved)
    first_products = (
        (enc_saved[10], 0, enc_branch, 0),
        (enc_saved[8], 0, enc_upper, 0),
    )
    if fast:
        first = Bucket(first_products)
        enc_upper, first.send = tie(enc_upper, first.send)
        first.pair_hop()
    grad_middle, enc_attn_branch, grad_attn, enc_norm_two = rest(enc_upper)
    enc_mixed = attn_backward(grad_attn, enc_saved, HEADS_ENC, HEADS_ENC)
    enc_mixed = enc_mixed.reshape(enc_saved[3].shape)
    second_products = (
        (enc_saved[5], 1, enc_attn_branch, 0),
        (enc_saved[2], 0, enc_mixed, 1),
        (dec_saved[2], 0, dec_mixed, 1),
        (latent_in, 0, grad_latent, 0),
        (None, None, dec_vec_grads, 0),
    )
    if fast:
        clock = first.first_hop(enc_mixed)
        enc_mixed, _ = tie(enc_mixed, early.third_hop(clock))
        second = Bucket(second_products)
        second.pair_hop()
        enc_mixed, _ = tie(enc_mixed, second.send)
    grad_tokens, enc_norm_one = input_backward(grad_middle, enc_mixed, enc_weights, enc_saved)
    grad_loc_row = grad_tokens[1:2]
    grad_loc = jnp.dot(grad_loc_row.T, time_loc, precision=lax.Precision.HIGHEST)
    grad_time = jnp.dot(grad_loc_row, loc_rows.T, precision=lax.Precision.HIGHEST)
    enc_vec_grads = columns(
        (grad_tokens[0], *enc_norm_one, *enc_norm_two, grad_loc), 2 * LANES
    ).astype(BF16)
    grad_raw = (grad_tokens / band_count).astype(BF16)
    third_products = (
        (grad_raw, 0, wave_pixels, 0),
        (None, None, enc_vec_grads, 0),
    )
    if fast:
        third = Bucket(third_products)
        third.pair_hop()
        grad_raw, _ = tie(grad_raw, third.send)
    grad_waves = dot(grad_raw[2:], table, 1, 0).astype(BF16)
    grad_chip = dot(grad_waves, spread, 1, 1).astype(BF16)
    here = grad_chip.shape[1] // 2
    mine, theirs = grad_chip[:, :here], swap(grad_chip[:, here:])
    grad_pixels = jnp.where(
        side == 0, jnp.stack([mine, theirs]), jnp.stack([theirs, mine])
    ).astype(F32)
    if fast:
        clock = second.first_hop(grad_chip)
        clock = early.fourth_hop(clock)
        clock = first.second_hop(clock)
        clock = third.first_hop(clock)
        early.arrived, clock = tie(early.arrived, clock)
        s_dec_down, s_dec_up, s_dec_out = early.finish()
        grad_pixels, s_dec_up = tie(grad_pixels, s_dec_up)
        clock = first.third_hop(s_dec_up)
        clock = second.second_hop(clock)
        clock = third.second_hop(clock)
        clock = first.fourth_hop(clock)
        clock = second.third_hop(clock)
        clock = third.third_hop(clock)
        clock = second.fourth_hop(clock)
        clock = third.fourth_hop(clock)
        s_enc_down, s_enc_up = first.finish()
        second_sums = second.finish()
        third_sums = third.finish()
    else:
        whole = lambda products: scatter_sums([
            right if left is None else dot(left, right, i, j).astype(BF16)
            for left, i, right, j in products
        ], device_count)
        s_dec_down, s_dec_up, s_dec_out = whole(dec_products)
        s_enc_down, s_enc_up = whole(first_products)
        second_sums, third_sums = whole(second_products), whole(third_products)
    s_enc_out, s_enc_qkv, s_dec_qkv, s_proj, s_dec_vec = second_sums
    s_table, s_enc_vec = third_sums
    return (
        decoded.astype(BF16)[None],
        grad_pixels,
        grad_time,
        s_table.reshape(band_table.shape),
        s_enc_vec[:, 0],
        s_enc_vec[:, 5 : 5 + loc_weight.shape[1]],
        s_enc_vec[:, 1],
        s_enc_vec[:, 2],
        s_enc_qkv,
        s_enc_out,
        s_enc_vec[:, 3],
        s_enc_vec[:, 4],
        s_enc_up,
        s_enc_down,
        s_proj,
        s_dec_vec[:, 0],
        s_dec_vec[:, 1],
        s_dec_vec[:, 2],
        s_dec_qkv,
        s_dec_out,
        s_dec_vec[:, 3],
        s_dec_vec[:, 4],
        s_dec_up,
        s_dec_down,
    )


def solution(mesh):
    dp, chip, both, matrix = P("dp"), P("dp", "band"), P(BOTH, None), P("dp", None)
    block = (dp, dp, matrix, matrix, dp, dp, matrix, matrix)
    in_specs = (
        P("dp", None, "band"), both, chip, chip, both,
        P("dp", None, None), dp, matrix, *block, matrix, dp, *block, P(BOTH, None, None),
    )
    out_specs = (
        P(BOTH, None, None), P("dp", None, "band"), both,
        P("dp", None, None), dp, matrix, *block, matrix, dp, *block,
    )
    return jax.shard_map(
        functools.partial(per_device, device_count=mesh.size),
        mesh=mesh, in_specs=in_specs, out_specs=out_specs, check_vma=False,
    )
```

```python
import functools
import math

import jax
import jax.numpy as jnp
from jax import lax
from jax.experimental import pallas as pl
from jax.experimental.pallas import tpu as pltpu
from jax.sharding import PartitionSpec as P

HEADS_ENC = 12
HEADS_DEC = 16
EPSILON = 1e-05
F32 = jnp.float32
BF16 = jnp.bfloat16
BOTH = ("dp", "band")


def dot(a, b, ca, cb):
    return lax.dot_general(a, b, (((ca,), (cb,)), ((), ())), preferred_element_type=F32)


def sincos(place_index, model_width):
    half_width = model_width // 2
    frequency = jnp.exp(-math.log(10000.0) * jnp.arange(half_width, dtype=F32) / half_width)
    angles = place_index[..., None] * frequency
    return jnp.concatenate([jnp.sin(angles), jnp.cos(angles)], -1)


def attend_forward_kernel(q_ref, k_ref, v_ref, out_ref, lse_ref, *, head_size, scale):
    log_scale = scale * math.log2(math.e)
    for first in range(0, q_ref.shape[0], head_size):
        rows = slice(first, first + head_size)
        scores = dot(k_ref[rows], q_ref[rows], 0, 0)
        top = jnp.max(scores, axis=0, keepdims=True) * log_scale
        weights = jnp.exp2(scores * log_scale - top)
        total = jnp.sum(weights, axis=0, keepdims=True)
        mixed = dot(v_ref[rows], weights.astype(BF16), 1, 0)
        out_ref[rows] = (mixed / total).astype(BF16)
        lse_ref[first // head_size] = top + jnp.log2(total)


def attend_forward(mixed_rows, head_count, heads_a_step):
    triple, length = mixed_rows.shape
    width = triple // 3
    head_size = width // head_count
    steps = head_count // heads_a_step
    slab = heads_a_step * head_size
    part = lambda which: pl.BlockSpec((slab, length), lambda h: (which * steps + h, 0))
    return pl.pallas_call(
        functools.partial(attend_forward_kernel, head_size=head_size, scale=head_size**-0.5),
        grid=(steps,),
        in_specs=[part(0), part(1), part(2)],
        out_specs=[part(0), pl.BlockSpec((heads_a_step, 1, length), lambda h: (h, 0, 0))],
        out_shape=[
            jax.ShapeDtypeStruct((width, length), BF16),
            jax.ShapeDtypeStruct((head_count, 1, length), F32),
        ],
        compiler_params=pltpu.CompilerParams(vmem_limit_bytes=40 << 20),
    )(mixed_rows, mixed_rows, mixed_rows)


def attend_backward_kernel(
    q_ref, k_ref, v_ref, out_ref, grad_ref, lse_ref, *rest, head_size, scale
):
    grad_mixed_ref = rest[-1]
    log_scale = scale * math.log2(math.e)
    for first in range(0, q_ref.shape[0], head_size):
        rows = slice(first, first + head_size)
        q, k, v, grad = q_ref[rows], k_ref[rows], v_ref[rows], grad_ref[rows]
        delta = jnp.sum(grad.astype(F32) * out_ref[rows].astype(F32), axis=0, keepdims=True)
        probs = jnp.exp2(dot(k, q, 0, 0) * log_scale - lse_ref[first // head_size])
        grad_probs = dot(v, grad, 0, 0)
        grad_scores = (probs * (grad_probs - delta)).astype(BF16)
        grad_mixed_ref[0, rows] = (dot(k, grad_scores, 1, 0) * scale).astype(BF16)
        grad_mixed_ref[1, rows] = (dot(q, grad_scores, 1, 1) * scale).astype(BF16)
        grad_mixed_ref[2, rows] = dot(grad, probs.astype(BF16), 1, 1).astype(BF16)


def attend_backward(
    mixed_rows, out_rows, grad_rows, lse, head_count, heads_a_step, share=(0, 1), before=None
):
    triple, length = mixed_rows.shape
    width = triple // 3
    head_size = width // head_count
    total = head_count // heads_a_step
    steps = total // share[1]
    start = share[0] * steps
    slab = heads_a_step * head_size
    part = lambda which: pl.BlockSpec((slab, length), lambda h: (which * total + start + h, 0))
    extra = [] if before is None else [before]
    return pl.pallas_call(
        functools.partial(attend_backward_kernel, head_size=head_size, scale=head_size**-0.5),
        grid=(steps,),
        in_specs=[
            part(0),
            part(1),
            part(2),
            part(0),
            part(0),
            pl.BlockSpec((heads_a_step, 1, length), lambda h: (start + h, 0, 0)),
        ]
        + [pl.BlockSpec(memory_space=pl.ANY) for _ in extra],
        out_specs=pl.BlockSpec((3, slab, length), lambda h: (0, start + h, 0)),
        out_shape=jax.ShapeDtypeStruct((3, width, length), BF16),
        input_output_aliases={6: 0} if extra else {},
        compiler_params=pltpu.CompilerParams(vmem_limit_bytes=40 << 20),
    )(mixed_rows, mixed_rows, mixed_rows, out_rows, grad_rows, lse, *extra)


def norm_forward(rows_in, gain_row, shift_row):
    centred = rows_in - jnp.mean(rows_in, -1, keepdims=True)
    inverse = lax.rsqrt(jnp.mean(centred * centred, -1, keepdims=True) + EPSILON)
    unit_rows = centred * inverse
    return (unit_rows * gain_row + shift_row).astype(BF16), unit_rows, inverse


def norm_backward(grad_normed, unit_rows, inverse, gain_row):
    grad_unit = grad_normed * gain_row
    grad_input = inverse * (
        grad_unit
        - jnp.mean(grad_unit, -1, keepdims=True)
        - unit_rows * jnp.mean(grad_unit * unit_rows, -1, keepdims=True)
    )
    return grad_input, jnp.sum(grad_normed * unit_rows, 0), jnp.sum(grad_normed, 0)


def gelu_tanh(upper):
    return jax.nn.gelu(upper, approximate=True)


def attn_half(rows_in, gain_one, shift_one, w_qkv, w_out, head_count, heads_a_step):
    normed_one, unit_one, inverse_one = norm_forward(rows_in, gain_one, shift_one)
    mixed_rows = dot(w_qkv, normed_one, 0, 1).astype(BF16)
    attn_rows, lse = attend_forward(mixed_rows, head_count, heads_a_step)
    middle = rows_in + dot(attn_rows, w_out, 0, 0)
    return middle, (unit_one, inverse_one, normed_one, mixed_rows, lse, attn_rows)


def mlp_half(middle, saved, gain_two, shift_two, w_up, w_down):
    normed_two, unit_two, inverse_two = norm_forward(middle, gain_two, shift_two)
    upper = dot(normed_two, w_up, 1, 0)
    active = gelu_tanh(upper).astype(BF16)
    rows_out = middle + dot(active, w_down, 1, 0)
    return rows_out, saved + (unit_two, inverse_two, normed_two, upper, active)


def mlp_backward(grad_out, weights, saved):
    gain_two, w_out, w_up, w_down = weights[4], weights[3], weights[6], weights[7]
    unit_two, inverse_two, upper = saved[6], saved[7], saved[9]
    grad_branch = grad_out.astype(BF16)
    grad_active = dot(grad_branch, w_down, 1, 1)
    grad_upper = jax.vjp(gelu_tanh, upper)[1](grad_active)[0].astype(BF16)

    def rest(grad_upper):
        grad_normed = dot(grad_upper, w_up, 1, 1)
        grad_middle, grad_gain_two, grad_shift_two = norm_backward(
            grad_normed, unit_two, inverse_two, gain_two
        )
        grad_middle = grad_out + grad_middle
        grad_attn_branch = grad_middle.astype(BF16)
        grad_attn = dot(w_out, grad_attn_branch, 1, 1).astype(BF16)
        return grad_middle, grad_attn_branch, grad_attn, (grad_gain_two, grad_shift_two)

    return grad_branch, grad_upper, rest


def attn_backward(grad_attn, saved, head_count, heads_a_step, share=(0, 1), before=None):
    return attend_backward(
        saved[3], saved[5], grad_attn, saved[4], head_count, heads_a_step, share, before
    )


def input_backward(grad_middle, grad_mixed, weights, saved):
    grad_normed_one = dot(grad_mixed, weights[2], 0, 1)
    grad_input, grad_gain_one, grad_shift_one = norm_backward(
        grad_normed_one, saved[0], saved[1], weights[0]
    )
    return grad_middle + grad_input, (grad_gain_one, grad_shift_one)


def swap(array):
    return lax.ppermute(array, "band", [(0, 1), (1, 0)])


def join_pair(mine, axis):
    first = lax.axis_index("band") == 0
    other = swap(mine)
    return jnp.concatenate([jnp.where(first, mine, other), jnp.where(first, other, mine)], axis)


def groups_of(shards):
    rows = 0
    for shard in shards:
        rows = math.gcd(rows, shard.shape[0] // 2)
    return rows


def pack_rows(array, rows):
    lead, (length, width) = array.shape[:-2], array.shape[-2:]
    array = array.reshape(*lead, length // rows, rows, width)
    return jnp.swapaxes(array, -3, -2).reshape(*lead, rows, length // rows * width)


def unpack_rows(array, width):
    lead, (rows, total) = array.shape[:-2], array.shape[-2:]
    array = array.reshape(*lead, rows, total // width, width)
    return jnp.swapaxes(array, -3, -2).reshape(*lead, rows * (total // width), width)


def gather_all(shards):
    rows = groups_of(shards)
    side = lax.axis_index("band")
    halves = [
        lax.dynamic_slice_in_dim(s, side * (s.shape[0] // 2), s.shape[0] // 2, 0) for s in shards
    ]
    packed = jnp.concatenate([pack_rows(h, rows) for h in halves], 1)
    whole = lax.all_gather(packed, BOTH, axis=0, tiled=False)
    out, at = [], 0
    for half in halves:
        span = half.size // rows
        piece = unpack_rows(whole[:, :, at : at + span], half.shape[1])
        out.append(piece.reshape(-1, half.shape[1]))
        at += span
    return out


def pack_grads(grads, device_count):
    split = [g.reshape(device_count, -1, g.shape[1]) for g in grads]
    rows = 0
    for s in split:
        rows = math.gcd(rows, s.shape[1])
    return jnp.concatenate([pack_rows(s, rows) for s in split], 2)


def unpack_sums(summed, shapes):
    both = join_pair(summed[None], 0)
    rows = both.shape[1]
    out, at = [], 0
    for length, width in shapes:
        span = length // 2 * width // rows
        piece = unpack_rows(both[:, :, at : at + span], width)
        out.append(piece.reshape(length, width).astype(F32))
        at += span
    return out


def scatter_sums(grads, device_count):
    packed = pack_grads(grads, device_count)
    summed = lax.psum_scatter(packed, BOTH, scatter_dimension=0, tiled=False)
    dp_count = device_count // 2
    return unpack_sums(summed, [(g.shape[0] // dp_count, g.shape[1]) for g in grads])


LANES = 128
TILE = 16


def columns(vectors, lanes=LANES):
    stacked = jnp.concatenate([v if v.ndim == 2 else v[:, None] for v in vectors], 1)
    return jnp.pad(stacked, ((0, 0), (0, lanes - stacked.shape[1])))


def hop(flips):
    return [
        (dp * 2 + band, (dp ^ flips[band]) * 2 + band) for dp in range(16) for band in range(2)
    ]


FIRST_HOP = hop((2, 1))
SECOND_HOP = hop((1, 2))


def places(shapes):
    out, at = [], 0
    for rows, half in shapes:
        out.append((rows, half, at))
        at += rows // TILE * half
    return out, at


def lay(dst, src, rows, half, at):
    for group in range(rows // TILE):
        dst[:, at + group * half : at + (group + 1) * half] = src[group * TILE : (group + 1) * TILE]


def products_of(jobs, spots, refs, which):
    ins = list(refs)
    for (left_axis, right_axis), spot in zip(jobs, spots):
        left = None if left_axis is None else ins.pop(0)
        right = ins.pop(0)
        half = spot[1]
        span = pl.ds(pl.multiple_of(which * half, 128), half)
        values = right[span] if right_axis == 1 else right[:, span]
        yield values if left is None else dot(left[...], values, left_axis, right_axis)


def send_kernel(scalars, *refs, jobs, spots):
    out = refs[-1]
    halves = products_of(jobs, spots, refs[:-1], 1 - scalars[0])
    for values, (rows, half, at) in zip(halves, spots):
        values = values.astype(BF16)
        for block in range(16):
            lay(out.at[block], values[block * rows : (block + 1) * rows], rows, half, at)


def keep_kernel(scalars, *refs, jobs, spots):
    count = len(spots)
    arrived, send, keep, landed, sem = refs[-count - 5 : -count]
    copy = pltpu.make_async_copy(arrived, landed, sem)
    copy.start()
    halves = products_of(jobs, spots, refs[: -count - 5], scalars[0])
    for values, held in zip(halves, refs[-count:]):
        held[...] = values.astype(F32)
    copy.wait()
    for held, (rows, half, at) in zip(refs[-count:], spots):
        for step in range(16):
            block = scalars[1 + step]
            out = (send if step < 8 else keep).at[step % 8]
            for group in range(rows // TILE):
                span = slice(at + group * half, at + (group + 1) * half)
                own = held[pl.ds(pl.multiple_of(block * rows + group * TILE, TILE), TILE)]
                out[:, span] = (own + landed[block, :, span].astype(F32)).astype(BF16)


def split_kernel(table, own_send, own_keep, recv_send, recv_keep, send, keep):
    send[...] = (own_send[...].astype(F32) + recv_send[...].astype(F32)).astype(BF16)
    keep[...] = (own_keep[...].astype(F32) + recv_keep[...].astype(F32)).astype(BF16)


def unpack_kernel(scalars, mine, theirs, *outs, spots):
    side = scalars[0]
    for source, which in ((mine, side), (theirs, 1 - side)):
        for out, (rows, half, at) in zip(outs, spots):
            for group in range(rows // TILE):
                span = slice(at + group * half, at + (group + 1) * half)
                lanes = pl.ds(pl.multiple_of(which * half, 128), half)
                out[group * TILE : (group + 1) * TILE, lanes] = source[:, span].astype(F32)


def grid_call(kernel, scalars, grid, in_specs, out_specs, out_shape, *args):
    return pl.pallas_call(
        kernel,
        grid_spec=pltpu.PrefetchScalarGridSpec(
            num_scalar_prefetch=1, grid=grid, in_specs=in_specs, out_specs=out_specs
        ),
        out_shape=out_shape,
        compiler_params=pltpu.CompilerParams(vmem_limit_bytes=40 << 20),
    )(scalars, *args)


def vmem_call(kernel, out_shape, *args, away=0, scratch_shapes=()):
    whole = pl.BlockSpec(memory_space=pltpu.VMEM)
    return pl.pallas_call(
        kernel,
        in_specs=[pl.BlockSpec(memory_space=pltpu.SMEM)]
        + [whole] * (len(args) - 1 - away)
        + [pl.BlockSpec(memory_space=pl.ANY)] * away,
        out_specs=[whole] * len(out_shape),
        out_shape=out_shape,
        scratch_shapes=scratch_shapes,
        compiler_params=pltpu.CompilerParams(vmem_limit_bytes=56 << 20),
    )(*args)


def assemble_kernel(scalars, *refs, spots):
    pieces, outs, sem = refs[:8], refs[8:-1], refs[-1]
    copies = []
    for index, piece in enumerate(pieces):
        line = scalars[1 + index]
        side = scalars[0] if index < 4 else 1 - scalars[0]
        for which, rows, first, half, at in spots:
            lanes = pl.ds(pl.multiple_of(side * half, 128), half)
            copies.append(
                pltpu.make_async_copy(
                    piece.at[:, :, at : at + half],
                    outs[which].at[:, line, first : first + rows, lanes],
                    sem,
                )
            )
    for copy in copies:
        copy.start()
    for copy in copies:
        copy.wait()


class Gather:
    def __init__(self, shards, rows):
        dp, side = lax.axis_index("dp"), lax.axis_index("band")
        self.x, self.y, self.z, self.side = dp % 2, dp // 2 % 2, dp // 4, side
        self.shapes, self.spots, parts, at = [], [], [], 0
        for which, shard in enumerate(shards):
            length, width = shard.shape
            half = width // 2
            mine = lax.dynamic_slice_in_dim(shard, side * half, half, 1)
            for first in range(0, length, rows):
                parts.append(mine[first : first + rows])
                self.spots.append((which, rows, first, half, at))
                at += half
            self.shapes.append((4, 4, length, width))
        self.one = jnp.concatenate(parts, 1)

    def far_line(self):
        self.arrived = lax.ppermute(self.one, BOTH, hop((8, 8)))
        return self.one

    def near_line(self, clock):
        self.arrived, clock = tie(self.arrived, clock)
        low = self.z < 2
        self.two = jnp.stack(
            [jnp.where(low, self.one, self.arrived), jnp.where(low, self.arrived, self.one)]
        )
        self.arrived = lax.ppermute(self.two, BOTH, hop((4, 4)))
        return self.two

    def plane(self, clock):
        self.arrived, clock = tie(self.arrived, clock)
        even = self.z % 2 == 0
        four = jnp.stack(
            [jnp.where(even, self.two, self.arrived), jnp.where(even, self.arrived, self.two)], 1
        )
        own = four.reshape(4, *self.one.shape)
        self.pieces = [own, lax.ppermute(own, BOTH, SECOND_HOP), lax.ppermute(own, BOTH, FIRST_HOP)]
        self.partner = [swap(own)]
        return own

    def corner(self, clock):
        self.pieces[1], clock = tie(self.pieces[1], clock)
        self.pieces.append(lax.ppermute(self.pieces[1], BOTH, FIRST_HOP))
        self.partner.append(swap(self.pieces[1]))
        return self.pieces[1]

    def pair(self, clock):
        self.pieces[2:], clock = tie(self.pieces[2:], clock)
        self.partner += [swap(piece) for piece in self.pieces[2:]]
        return self.pieces[3]

    def weights(self):
        place = lambda x, y: y * 2 + x
        here, across, corner = (
            place(self.x, self.y), place(1 - self.x, self.y), place(1 - self.x, 1 - self.y)
        )
        along = place(self.x, 1 - self.y)
        first = self.side == 0
        one, two = jnp.where(first, across, along), jnp.where(first, along, across)
        table = jnp.stack([self.side, here, one, two, corner, here, two, one, corner])
        outs = vmem_call(
            functools.partial(assemble_kernel, spots=self.spots),
            [jax.ShapeDtypeStruct(shape, BF16) for shape in self.shapes],
            table.astype(jnp.int32),
            *self.pieces,
            *self.partner,
            away=8,
            scratch_shapes=[pltpu.SemaphoreType.DMA(())],
        )
        return [out.reshape(-1, out.shape[3]) for out in outs]


class Bucket:
    def __init__(self, products):
        dp, side = lax.axis_index("dp"), lax.axis_index("band")
        self.x, self.y, self.z, self.side = dp % 2, dp // 2 % 2, dp // 4, side
        self.scalars = side[None].astype(jnp.int32)
        shapes, self.jobs, self.args = [], [], []
        for left, left_axis, right, right_axis in products:
            length = right.shape[0] if left is None else left.shape[1 - left_axis]
            shapes.append((length // 16, right.shape[1 - right_axis] // 2))
            self.jobs.append((left_axis, right_axis))
            self.args += [right] if left is None else [left, right]
        self.spots, self.total = places(shapes)
        (self.send,) = vmem_call(
            functools.partial(send_kernel, jobs=self.jobs, spots=self.spots),
            [self.shaped(16)],
            self.scalars,
            *self.args,
        )

    def shaped(self, count):
        return jax.ShapeDtypeStruct((count, TILE, self.total), BF16)

    def block(self, index):
        return pl.BlockSpec((1, TILE, self.total), index)

    def split(self, count, table, goes, stays):
        goes, stays, out = self.block(goes), self.block(stays), self.block(lambda i, t: (i, 0, 0))
        self.send, self.keep = grid_call(
            split_kernel,
            table.astype(jnp.int32),
            (count,),
            [goes, stays, goes, stays],
            [out] * 2,
            [self.shaped(count)] * 2,
            self.keep,
            self.keep,
            self.arrived,
            self.arrived,
        )

    def pair_hop(self):
        self.arrived = swap(self.send)

    def first_hop(self, clock):
        self.arrived, clock = tie(self.arrived, clock)
        line = jnp.arange(8, dtype=jnp.int32)
        z, other = line // 2, line % 2
        near = jnp.where(self.side == 0, self.y, self.x)
        place = lambda bit: z * 4 + jnp.where(self.side == 0, bit * 2 + other, other * 2 + bit)
        table = jnp.concatenate([self.side[None], place(1 - near), place(near)])
        self.send, self.keep = vmem_call(
            functools.partial(keep_kernel, jobs=self.jobs, spots=self.spots),
            [self.shaped(8)] * 2,
            table.astype(jnp.int32),
            *self.args,
            self.arrived,
            away=1,
            scratch_shapes=[pltpu.VMEM((16, TILE, self.total), BF16), pltpu.SemaphoreType.DMA(())]
            + [pltpu.VMEM((16 * rows, half), F32) for rows, half, _ in self.spots],
        )
        self.arrived = lax.ppermute(self.send, BOTH, FIRST_HOP)
        return self.send

    def later_hop(self, clock, count, bit, pairs):
        self.arrived, clock = tie(self.arrived, clock)
        self.split(
            count,
            bit[None],
            lambda i, t: (2 * i + 1 - t[0], 0, 0),
            lambda i, t: (2 * i + t[0], 0, 0),
        )
        self.arrived = lax.ppermute(self.send, BOTH, pairs)
        return self.send

    def second_hop(self, clock):
        far = jnp.where(self.side == 0, self.x, self.y)
        return self.later_hop(clock, 4, far, SECOND_HOP)

    def third_hop(self, clock):
        return self.later_hop(clock, 2, self.z % 2, hop((4, 4)))

    def fourth_hop(self, clock):
        return self.later_hop(clock, 1, self.z // 2, hop((8, 8)))

    def finish(self):
        mine = (self.keep[0].astype(F32) + self.arrived[0].astype(F32)).astype(BF16)
        return vmem_call(
            functools.partial(unpack_kernel, spots=self.spots),
            [jax.ShapeDtypeStruct((r, 2 * h), F32) for r, h, _ in self.spots],
            self.scalars,
            mine,
            swap(mine),
        )


def tie(first, second):
    return lax.optimization_barrier((first, second))


def per_device(
    pixels, time_loc, band_mask, wavelengths, visible, band_table, cls_token, loc_weight,
    enc_attn_gain, enc_attn_shift, enc_qkv, enc_out, enc_mlp_gain, enc_mlp_shift, enc_up, enc_down,
    projection, mask_token, dec_attn_gain, dec_attn_shift, dec_qkv, dec_out, dec_mlp_gain,
    dec_mlp_shift, dec_up, dec_down, cotangent, *, device_count,
):
    side = lax.axis_index("band")
    table_rows = band_table.shape[0]
    wave_count, pixel_size = band_table.shape[1:]
    fast = device_count == 32
    enc_vectors = columns(
        [cls_token, enc_attn_gain, enc_attn_shift, enc_mlp_gain, enc_mlp_shift, loc_weight], 2 * LANES
    )
    dec_vectors = columns(
        [mask_token, dec_attn_gain, dec_attn_shift, dec_mlp_gain, dec_mlp_shift], 2 * LANES
    )
    shards = (
        [band_table.reshape(table_rows, -1), enc_vectors, enc_qkv, enc_out],
        [enc_up, enc_down, projection],
        [dec_vectors, dec_qkv, dec_out, dec_up, dec_down],
    )
    if fast:
        front, middle, back = (Gather(group, group[0].shape[0]) for group in shards)
        clock = front.far_line()
        clock = front.near_line(clock)
        middle.one, clock = tie(middle.one, clock)
        clock = middle.far_line()
        clock = front.plane(clock)
        clock = middle.near_line(clock)
        back.one, clock = tie(back.one, clock)
        clock = back.far_line()
        clock = front.corner(clock)
        clock = middle.plane(clock)
        clock = back.near_line(clock)
        clock = front.pair(clock)
        groups = [front.weights()]
    else:
        weights = gather_all([shard for group in shards for shard in group])
        groups = [weights[:4], weights[4:7], weights[7:]]
    table, enc_vectors, w_enc_qkv, w_enc_out = groups[0]
    enc_vec = enc_vectors.T.astype(F32)
    loc_rows = enc_vec[5 : 5 + loc_weight.shape[1]]

    def own_chip(array):
        mine = lax.dynamic_index_in_dim(array, side, 0, keepdims=False)
        theirs = lax.dynamic_index_in_dim(array, 1 - side, 0, keepdims=False)
        return jnp.concatenate([mine, swap(theirs)], -1)

    chip_pixels = own_chip(pixels)
    chip_mask = own_chip(band_mask)
    chip_waves = own_chip(wavelengths)
    picks = visible[0]
    slot_wave = (chip_waves[:, None] == jnp.arange(wave_count, dtype=jnp.int32)) & (
        chip_mask[:, None] > 0
    )
    same_pixel = jnp.arange(pixel_size)[:, None] == jnp.arange(pixel_size)
    spread = (slot_wave[:, None, :, None] & same_pixel[None, :, None, :]).astype(BF16)
    spread = spread.reshape(chip_pixels.shape[1], wave_count * pixel_size)
    wave_pixels = jnp.pad(dot(chip_pixels, spread, 1, 0).astype(BF16), ((2, 0), (0, 0)))
    picks = jnp.pad(picks, (2, 0), constant_values=-1)
    band_count = jnp.sum(chip_mask).astype(F32)

    width = table.shape[0]
    patch_rows = dot(wave_pixels, table, 1, 1) / band_count + sincos(picks.astype(F32), width)
    loc_token = jnp.dot(time_loc, loc_rows, precision=lax.Precision.HIGHEST)
    tokens = jnp.concatenate([enc_vec[0:1], loc_token, patch_rows[2:]], 0)
    enc_half, enc_saved = attn_half(
        tokens, enc_vec[1], enc_vec[2], w_enc_qkv, w_enc_out, HEADS_ENC, HEADS_ENC
    )
    if fast:
        clock, enc_half = tie(clock, enc_half)
        clock = middle.corner(clock)
        clock = back.plane(clock)
        clock = middle.pair(clock)
        groups.append(middle.weights())
    w_enc_up, w_enc_down, w_proj = groups[1]
    enc_weights = (
        enc_vec[1], enc_vec[2], w_enc_qkv, w_enc_out, enc_vec[3], enc_vec[4], w_enc_up, w_enc_down
    )
    encoded, enc_saved = mlp_half(enc_half, enc_saved, *enc_weights[4:])
    latent_in = encoded.astype(BF16)
    latent = dot(latent_in, w_proj, 1, 0).astype(BF16)

    if fast:
        clock, latent = tie(clock, latent)
        clock = back.corner(clock)
        clock = back.pair(clock)
        groups.append(back.weights())
    dec_vectors, w_dec_qkv, w_dec_out, w_dec_up, w_dec_down = groups[2]
    dec_vec = dec_vectors.T.astype(F32)
    dec_weights = (
        dec_vec[1], dec_vec[2], w_dec_qkv, w_dec_out, dec_vec[3], dec_vec[4], w_dec_up, w_dec_down
    )
    positions = jnp.arange(cotangent.shape[1], dtype=jnp.int32)
    matches = positions[:, None] == picks[None, :]
    hidden = 1.0 - jnp.sum(matches.astype(F32), 1, keepdims=True)
    matches = matches.astype(BF16)
    inserted = (
        dot(matches, latent, 1, 0)
        + hidden * dec_vec[0]
        + sincos(positions.astype(F32), latent.shape[1])
    )
    dec_half, dec_saved = attn_half(inserted, *dec_weights[:4], HEADS_DEC, 1)
    decoded, dec_saved = mlp_half(dec_half, dec_saved, *dec_weights[4:])
    grad_out = cotangent[0].astype(F32)
    dec_branch, dec_upper, rest = mlp_backward(grad_out, dec_weights, dec_saved)
    grad_middle, dec_attn_branch, grad_attn, dec_norm_two = rest(dec_upper)
    dec_products = (
        (dec_saved[10], 0, dec_branch, 0),
        (dec_saved[8], 0, dec_upper, 0),
        (dec_saved[5], 1, dec_attn_branch, 0),
    )
    if fast:
        early = Bucket(dec_products)
        grad_attn, early.send = tie(grad_attn, early.send)
        early.pair_hop()
        dec_mixed = attn_backward(grad_attn, dec_saved, HEADS_DEC, 1, (0, 2))
        dec_mixed, early.send = tie(dec_mixed, early.first_hop(dec_mixed))
        dec_mixed = attn_backward(grad_attn, dec_saved, HEADS_DEC, 1, (1, 2), dec_mixed)
        dec_mixed, early.send = tie(dec_mixed, early.second_hop(dec_mixed))
    else:
        dec_mixed = attn_backward(grad_attn, dec_saved, HEADS_DEC, 1)
    dec_mixed = dec_mixed.reshape(dec_saved[3].shape)
    grad_inserted, dec_norm_one = input_backward(grad_middle, dec_mixed, dec_weights, dec_saved)
    grad_mask = jnp.sum(grad_inserted * hidden, 0)
    dec_vec_grads = columns((grad_mask, *dec_norm_one, *dec_norm_two), 2 * LANES).astype(BF16)
    grad_latent = dot(matches, grad_inserted.astype(BF16), 0, 0).astype(BF16)
    grad_encoded = dot(grad_latent, w_proj, 1, 1)

    enc_branch, enc_upper, rest = mlp_backward(grad_encoded, enc_weights, enc_saved)
    first_products = (
        (enc_saved[10], 0, enc_branch, 0),
        (enc_saved[8], 0, enc_upper, 0),
    )
    if fast:
        first = Bucket(first_products)
        enc_upper, first.send = tie(enc_upper, first.send)
        first.pair_hop()
    grad_middle, enc_attn_branch, grad_attn, enc_norm_two = rest(enc_upper)
    enc_mixed = attn_backward(grad_attn, enc_saved, HEADS_ENC, HEADS_ENC)
    enc_mixed = enc_mixed.reshape(enc_saved[3].shape)
    second_products = (
        (enc_saved[5], 1, enc_attn_branch, 0),
        (enc_saved[2], 0, enc_mixed, 1),
        (dec_saved[2], 0, dec_mixed, 1),
        (latent_in, 0, grad_latent, 0),
        (None, None, dec_vec_grads, 0),
    )
    if fast:
        clock = first.first_hop(enc_mixed)
        enc_mixed, _ = tie(enc_mixed, early.third_hop(clock))
        second = Bucket(second_products)
        second.pair_hop()
        enc_mixed, _ = tie(enc_mixed, second.send)
    grad_tokens, enc_norm_one = input_backward(grad_middle, enc_mixed, enc_weights, enc_saved)
    grad_loc_row = grad_tokens[1:2]
    grad_loc = jnp.dot(grad_loc_row.T, time_loc, precision=lax.Precision.HIGHEST)
    grad_time = jnp.dot(grad_loc_row, loc_rows.T, precision=lax.Precision.HIGHEST)
    enc_vec_grads = columns(
        (grad_tokens[0], *enc_norm_one, *enc_norm_two, grad_loc), 2 * LANES
    ).astype(BF16)
    grad_raw = (grad_tokens / band_count).astype(BF16)
    third_products = (
        (grad_raw, 0, wave_pixels, 0),
        (None, None, enc_vec_grads, 0),
    )
    if fast:
        third = Bucket(third_products)
        third.pair_hop()
        grad_raw, _ = tie(grad_raw, third.send)
    grad_waves = dot(grad_raw[2:], table, 1, 0).astype(BF16)
    grad_chip = dot(grad_waves, spread, 1, 1).astype(BF16)
    here = grad_chip.shape[1] // 2
    mine, theirs = grad_chip[:, :here], swap(grad_chip[:, here:])
    grad_pixels = jnp.where(
        side == 0, jnp.stack([mine, theirs]), jnp.stack([theirs, mine])
    ).astype(F32)
    if fast:
        clock = second.first_hop(grad_chip)
        clock = early.fourth_hop(clock)
        clock = first.second_hop(clock)
        clock = third.first_hop(clock)
        early.arrived, clock = tie(early.arrived, clock)
        s_dec_down, s_dec_up, s_dec_out = early.finish()
        grad_pixels, s_dec_up = tie(grad_pixels, s_dec_up)
        clock = first.third_hop(s_dec_up)
        clock = second.second_hop(clock)
        clock = third.second_hop(clock)
        clock = first.fourth_hop(clock)
        clock = second.third_hop(clock)
        clock = third.third_hop(clock)
        clock = second.fourth_hop(clock)
        clock = third.fourth_hop(clock)
        s_enc_down, s_enc_up = first.finish()
        second_sums = second.finish()
        third_sums = third.finish()
    else:
        whole = lambda products: scatter_sums([
            right if left is None else dot(left, right, i, j).astype(BF16)
            for left, i, right, j in products
        ], device_count)
        s_dec_down, s_dec_up, s_dec_out = whole(dec_products)
        s_enc_down, s_enc_up = whole(first_products)
        second_sums, third_sums = whole(second_products), whole(third_products)
    s_enc_out, s_enc_qkv, s_dec_qkv, s_proj, s_dec_vec = second_sums
    s_table, s_enc_vec = third_sums
    return (
        decoded.astype(BF16)[None],
        grad_pixels,
        grad_time,
        s_table.reshape(band_table.shape),
        s_enc_vec[:, 0],
        s_enc_vec[:, 5 : 5 + loc_weight.shape[1]],
        s_enc_vec[:, 1],
        s_enc_vec[:, 2],
        s_enc_qkv,
        s_enc_out,
        s_enc_vec[:, 3],
        s_enc_vec[:, 4],
        s_enc_up,
        s_enc_down,
        s_proj,
        s_dec_vec[:, 0],
        s_dec_vec[:, 1],
        s_dec_vec[:, 2],
        s_dec_qkv,
        s_dec_out,
        s_dec_vec[:, 3],
        s_dec_vec[:, 4],
        s_dec_up,
        s_dec_down,
    )


def solution(mesh):
    dp, chip, both, matrix = P("dp"), P("dp", "band"), P(BOTH, None), P("dp", None)
    block = (dp, dp, matrix, matrix, dp, dp, matrix, matrix)
    in_specs = (
        P("dp", None, "band"), both, chip, chip, both,
        P("dp", None, None), dp, matrix, *block, matrix, dp, *block, P(BOTH, None, None),
    )
    out_specs = (
        P(BOTH, None, None), P("dp", None, "band"), both,
        P("dp", None, None), dp, matrix, *block, matrix, dp, *block,
    )
    return jax.shard_map(
        functools.partial(per_device, device_count=mesh.size),
        mesh=mesh, in_specs=in_specs, out_specs=out_specs, check_vma=False,
    )
```

```python
import functools
import math

import jax
import jax.numpy as jnp
from jax import lax
from jax.experimental import pallas as pl
from jax.experimental.pallas import tpu as pltpu
from jax.sharding import PartitionSpec as P

HEADS_ENC = 12
HEADS_DEC = 16
EPSILON = 1e-05
F32 = jnp.float32
BF16 = jnp.bfloat16
BOTH = ("dp", "band")


def dot(a, b, ca, cb):
    return lax.dot_general(a, b, (((ca,), (cb,)), ((), ())), preferred_element_type=F32)


def sincos(place_index, model_width):
    half_width = model_width // 2
    frequency = jnp.exp(-math.log(10000.0) * jnp.arange(half_width, dtype=F32) / half_width)
    angles = place_index[..., None] * frequency
    return jnp.concatenate([jnp.sin(angles), jnp.cos(angles)], -1)


def attend_forward_kernel(q_ref, k_ref, v_ref, out_ref, lse_ref, *, head_size, scale):
    log_scale = scale * math.log2(math.e)
    for first in range(0, q_ref.shape[0], head_size):
        rows = slice(first, first + head_size)
        scores = dot(k_ref[rows], q_ref[rows], 0, 0)
        top = jnp.max(scores, axis=0, keepdims=True) * log_scale
        weights = jnp.exp2(scores * log_scale - top)
        total = jnp.sum(weights, axis=0, keepdims=True)
        mixed = dot(v_ref[rows], weights.astype(BF16), 1, 0)
        out_ref[rows] = (mixed / total).astype(BF16)
        lse_ref[first // head_size] = top + jnp.log2(total)


def attend_forward(mixed_rows, head_count, heads_a_step):
    triple, length = mixed_rows.shape
    width = triple // 3
    head_size = width // head_count
    steps = head_count // heads_a_step
    slab = heads_a_step * head_size
    part = lambda which: pl.BlockSpec((slab, length), lambda h: (which * steps + h, 0))
    return pl.pallas_call(
        functools.partial(attend_forward_kernel, head_size=head_size, scale=head_size**-0.5),
        grid=(steps,),
        in_specs=[part(0), part(1), part(2)],
        out_specs=[part(0), pl.BlockSpec((heads_a_step, 1, length), lambda h: (h, 0, 0))],
        out_shape=[
            jax.ShapeDtypeStruct((width, length), BF16),
            jax.ShapeDtypeStruct((head_count, 1, length), F32),
        ],
        compiler_params=pltpu.CompilerParams(vmem_limit_bytes=40 << 20),
    )(mixed_rows, mixed_rows, mixed_rows)


def attend_backward_kernel(
    q_ref, k_ref, v_ref, out_ref, grad_ref, lse_ref, *rest, head_size, scale
):
    grad_mixed_ref = rest[-1]
    log_scale = scale * math.log2(math.e)
    for first in range(0, q_ref.shape[0], head_size):
        rows = slice(first, first + head_size)
        q, k, v, grad = q_ref[rows], k_ref[rows], v_ref[rows], grad_ref[rows]
        delta = jnp.sum(grad.astype(F32) * out_ref[rows].astype(F32), axis=0, keepdims=True)
        probs = jnp.exp2(dot(k, q, 0, 0) * log_scale - lse_ref[first // head_size])
        grad_probs = dot(v, grad, 0, 0)
        grad_scores = (probs * (grad_probs - delta)).astype(BF16)
        grad_mixed_ref[0, rows] = (dot(k, grad_scores, 1, 0) * scale).astype(BF16)
        grad_mixed_ref[1, rows] = (dot(q, grad_scores, 1, 1) * scale).astype(BF16)
        grad_mixed_ref[2, rows] = dot(grad, probs.astype(BF16), 1, 1).astype(BF16)


def attend_backward(
    mixed_rows, out_rows, grad_rows, lse, head_count, heads_a_step, share=(0, 1), before=None
):
    triple, length = mixed_rows.shape
    width = triple // 3
    head_size = width // head_count
    total = head_count // heads_a_step
    steps = total // share[1]
    start = share[0] * steps
    slab = heads_a_step * head_size
    part = lambda which: pl.BlockSpec((slab, length), lambda h: (which * total + start + h, 0))
    extra = [] if before is None else [before]
    return pl.pallas_call(
        functools.partial(attend_backward_kernel, head_size=head_size, scale=head_size**-0.5),
        grid=(steps,),
        in_specs=[
            part(0),
            part(1),
            part(2),
            part(0),
            part(0),
            pl.BlockSpec((heads_a_step, 1, length), lambda h: (start + h, 0, 0)),
        ]
        + [pl.BlockSpec(memory_space=pl.ANY) for _ in extra],
        out_specs=pl.BlockSpec((3, slab, length), lambda h: (0, start + h, 0)),
        out_shape=jax.ShapeDtypeStruct((3, width, length), BF16),
        input_output_aliases={6: 0} if extra else {},
        compiler_params=pltpu.CompilerParams(vmem_limit_bytes=40 << 20),
    )(mixed_rows, mixed_rows, mixed_rows, out_rows, grad_rows, lse, *extra)


def norm_forward(rows_in, gain_row, shift_row):
    centred = rows_in - jnp.mean(rows_in, -1, keepdims=True)
    inverse = lax.rsqrt(jnp.mean(centred * centred, -1, keepdims=True) + EPSILON)
    unit_rows = centred * inverse
    return (unit_rows * gain_row + shift_row).astype(BF16), unit_rows, inverse


def norm_backward(grad_normed, unit_rows, inverse, gain_row):
    grad_unit = grad_normed * gain_row
    grad_input = inverse * (
        grad_unit
        - jnp.mean(grad_unit, -1, keepdims=True)
        - unit_rows * jnp.mean(grad_unit * unit_rows, -1, keepdims=True)
    )
    return grad_input, jnp.sum(grad_normed * unit_rows, 0), jnp.sum(grad_normed, 0)


def gelu_tanh(upper):
    return jax.nn.gelu(upper, approximate=True)


def attn_half(rows_in, gain_one, shift_one, w_qkv, w_out, head_count, heads_a_step):
    normed_one, unit_one, inverse_one = norm_forward(rows_in, gain_one, shift_one)
    mixed_rows = dot(w_qkv, normed_one, 0, 1).astype(BF16)
    attn_rows, lse = attend_forward(mixed_rows, head_count, heads_a_step)
    middle = rows_in + dot(attn_rows, w_out, 0, 0)
    return middle, (unit_one, inverse_one, normed_one, mixed_rows, lse, attn_rows)


def mlp_half(middle, saved, gain_two, shift_two, w_up, w_down):
    normed_two, unit_two, inverse_two = norm_forward(middle, gain_two, shift_two)
    upper = dot(normed_two, w_up, 1, 0)
    active = gelu_tanh(upper).astype(BF16)
    rows_out = middle + dot(active, w_down, 1, 0)
    return rows_out, saved + (unit_two, inverse_two, normed_two, upper, active)


def mlp_backward(grad_out, weights, saved):
    gain_two, w_out, w_up, w_down = weights[4], weights[3], weights[6], weights[7]
    unit_two, inverse_two, upper = saved[6], saved[7], saved[9]
    grad_branch = grad_out.astype(BF16)
    grad_active = dot(grad_branch, w_down, 1, 1)
    grad_upper = jax.vjp(gelu_tanh, upper)[1](grad_active)[0].astype(BF16)

    def rest(grad_upper):
        grad_normed = dot(grad_upper, w_up, 1, 1)
        grad_middle, grad_gain_two, grad_shift_two = norm_backward(
            grad_normed, unit_two, inverse_two, gain_two
        )
        grad_middle = grad_out + grad_middle
        grad_attn_branch = grad_middle.astype(BF16)
        grad_attn = dot(w_out, grad_attn_branch, 1, 1).astype(BF16)
        return grad_middle, grad_attn_branch, grad_attn, (grad_gain_two, grad_shift_two)

    return grad_branch, grad_upper, rest


def attn_backward(grad_attn, saved, head_count, heads_a_step, share=(0, 1), before=None):
    return attend_backward(
        saved[3], saved[5], grad_attn, saved[4], head_count, heads_a_step, share, before
    )


def input_backward(grad_middle, grad_mixed, weights, saved):
    grad_normed_one = dot(grad_mixed, weights[2], 0, 1)
    grad_input, grad_gain_one, grad_shift_one = norm_backward(
        grad_normed_one, saved[0], saved[1], weights[0]
    )
    return grad_middle + grad_input, (grad_gain_one, grad_shift_one)


def swap(array):
    return lax.ppermute(array, "band", [(0, 1), (1, 0)])


def join_pair(mine, axis):
    first = lax.axis_index("band") == 0
    other = swap(mine)
    return jnp.concatenate([jnp.where(first, mine, other), jnp.where(first, other, mine)], axis)


def groups_of(shards):
    rows = 0
    for shard in shards:
        rows = math.gcd(rows, shard.shape[0] // 2)
    return rows


def pack_rows(array, rows):
    lead, (length, width) = array.shape[:-2], array.shape[-2:]
    array = array.reshape(*lead, length // rows, rows, width)
    return jnp.swapaxes(array, -3, -2).reshape(*lead, rows, length // rows * width)


def unpack_rows(array, width):
    lead, (rows, total) = array.shape[:-2], array.shape[-2:]
    array = array.reshape(*lead, rows, total // width, width)
    return jnp.swapaxes(array, -3, -2).reshape(*lead, rows * (total // width), width)


def gather_all(shards):
    rows = groups_of(shards)
    side = lax.axis_index("band")
    halves = [
        lax.dynamic_slice_in_dim(s, side * (s.shape[0] // 2), s.shape[0] // 2, 0) for s in shards
    ]
    packed = jnp.concatenate([pack_rows(h, rows) for h in halves], 1)
    whole = lax.all_gather(packed, BOTH, axis=0, tiled=False)
    out, at = [], 0
    for half in halves:
        span = half.size // rows
        piece = unpack_rows(whole[:, :, at : at + span], half.shape[1])
        out.append(piece.reshape(-1, half.shape[1]))
        at += span
    return out


def pack_grads(grads, device_count):
    split = [g.reshape(device_count, -1, g.shape[1]) for g in grads]
    rows = 0
    for s in split:
        rows = math.gcd(rows, s.shape[1])
    return jnp.concatenate([pack_rows(s, rows) for s in split], 2)


def unpack_sums(summed, shapes):
    both = join_pair(summed[None], 0)
    rows = both.shape[1]
    out, at = [], 0
    for length, width in shapes:
        span = length // 2 * width // rows
        piece = unpack_rows(both[:, :, at : at + span], width)
        out.append(piece.reshape(length, width).astype(F32))
        at += span
    return out


def scatter_sums(grads, device_count):
    packed = pack_grads(grads, device_count)
    summed = lax.psum_scatter(packed, BOTH, scatter_dimension=0, tiled=False)
    dp_count = device_count // 2
    return unpack_sums(summed, [(g.shape[0] // dp_count, g.shape[1]) for g in grads])


LANES = 128
TILE = 16


def columns(vectors, lanes=LANES):
    stacked = jnp.concatenate([v if v.ndim == 2 else v[:, None] for v in vectors], 1)
    return jnp.pad(stacked, ((0, 0), (0, lanes - stacked.shape[1])))


def vector_rows(vectors):
    stacked = jnp.stack(vectors)
    return jnp.pad(stacked, ((0, TILE - stacked.shape[0]), (0, 0))).astype(BF16)


def hop(flips):
    return [
        (dp * 2 + band, (dp ^ flips[band]) * 2 + band) for dp in range(16) for band in range(2)
    ]


FIRST_HOP = hop((2, 1))
SECOND_HOP = hop((1, 2))


def places(shapes):
    out, at = [], 0
    for rows, half in shapes:
        out.append((rows, half, at))
        at += rows // TILE * half
    return out, at


def lay(dst, src, rows, half, at):
    for group in range(rows // TILE):
        dst[:, at + group * half : at + (group + 1) * half] = src[group * TILE : (group + 1) * TILE]


def products_of(jobs, spots, refs, which):
    ins = list(refs)
    for (left_axis, right_axis), spot in zip(jobs, spots):
        left, right = ins.pop(0), ins.pop(0)
        half = spot[1]
        span = pl.ds(pl.multiple_of(which * half, 128), half)
        values = right[span] if right_axis == 1 else right[:, span]
        yield dot(left[...], values, left_axis, right_axis)


def send_kernel(scalars, *refs, jobs, spots):
    out = refs[-1]
    halves = products_of(jobs, spots, refs[:-1], 1 - scalars[0])
    for values, (rows, half, at) in zip(halves, spots):
        values = values.astype(BF16)
        for block in range(16):
            lay(out.at[block], values[block * rows : (block + 1) * rows], rows, half, at)


def keep_kernel(scalars, *refs, jobs, spots):
    count = len(spots)
    arrived, send, keep, landed, sem = refs[-count - 5 : -count]
    copy = pltpu.make_async_copy(arrived, landed, sem)
    copy.start()
    halves = products_of(jobs, spots, refs[: -count - 5], scalars[0])
    for values, held in zip(halves, refs[-count:]):
        held[...] = values.astype(F32)
    copy.wait()
    for held, (rows, half, at) in zip(refs[-count:], spots):
        for step in range(16):
            block = scalars[1 + step]
            out = (send if step < 8 else keep).at[step % 8]
            for group in range(rows // TILE):
                span = slice(at + group * half, at + (group + 1) * half)
                own = held[pl.ds(pl.multiple_of(block * rows + group * TILE, TILE), TILE)]
                out[:, span] = (own + landed[block, :, span].astype(F32)).astype(BF16)


def split_kernel(table, own_send, own_keep, recv_send, recv_keep, send, keep):
    send[...] = (own_send[...].astype(F32) + recv_send[...].astype(F32)).astype(BF16)
    keep[...] = (own_keep[...].astype(F32) + recv_keep[...].astype(F32)).astype(BF16)


def unpack_kernel(scalars, mine, theirs, *outs, spots):
    side = scalars[0]
    for source, which in ((mine, side), (theirs, 1 - side)):
        for out, (rows, half, at) in zip(outs, spots):
            for group in range(rows // TILE):
                span = slice(at + group * half, at + (group + 1) * half)
                lanes = pl.ds(pl.multiple_of(which * half, 128), half)
                out[group * TILE : (group + 1) * TILE, lanes] = source[:, span].astype(F32)


def without(kernel, start, count):
    return lambda *refs: kernel(*refs[:start], *refs[start + count :])


def grid_call(kernel, scalars, grid, in_specs, out_specs, out_shape, *args, after=()):
    away = [pl.BlockSpec(memory_space=pl.ANY)] * len(after)
    return pl.pallas_call(
        without(kernel, 1 + len(args), len(after)),
        grid_spec=pltpu.PrefetchScalarGridSpec(
            num_scalar_prefetch=1, grid=grid, in_specs=in_specs + away, out_specs=out_specs
        ),
        out_shape=out_shape,
        compiler_params=pltpu.CompilerParams(vmem_limit_bytes=40 << 20),
    )(scalars, *args, *after)


def vmem_call(kernel, out_shape, *args, away=0, scratch_shapes=(), after=()):
    whole = pl.BlockSpec(memory_space=pltpu.VMEM)
    return pl.pallas_call(
        without(kernel, len(args), len(after)),
        in_specs=[pl.BlockSpec(memory_space=pltpu.SMEM)]
        + [whole] * (len(args) - 1 - away)
        + [pl.BlockSpec(memory_space=pl.ANY)] * (away + len(after)),
        out_specs=[whole] * len(out_shape),
        out_shape=out_shape,
        scratch_shapes=scratch_shapes,
        compiler_params=pltpu.CompilerParams(vmem_limit_bytes=56 << 20),
    )(*args, *after)


def assemble_kernel(scalars, *refs, spots):
    pieces, outs, sem = refs[:8], refs[8:-1], refs[-1]
    copies = []
    for index, piece in enumerate(pieces):
        line = scalars[1 + index]
        side = scalars[0] if index < 4 else 1 - scalars[0]
        for which, rows, first, half, at in spots:
            lanes = pl.ds(pl.multiple_of(side * half, 128), half)
            copies.append(
                pltpu.make_async_copy(
                    piece.at[:, :, at : at + half],
                    outs[which].at[:, line, first : first + rows, lanes],
                    sem,
                )
            )
    for copy in copies:
        copy.start()
    for copy in copies:
        copy.wait()


class Gather:
    def __init__(self, shards, rows):
        dp, side = lax.axis_index("dp"), lax.axis_index("band")
        self.x, self.y, self.z, self.side = dp % 2, dp // 2 % 2, dp // 4, side
        self.shapes, self.spots, parts, at = [], [], [], 0
        for which, shard in enumerate(shards):
            length, width = shard.shape
            half = width // 2
            mine = lax.dynamic_slice_in_dim(shard, side * half, half, 1)
            for first in range(0, length, rows):
                parts.append(mine[first : first + rows])
                self.spots.append((which, rows, first, half, at))
                at += half
            self.shapes.append((4, 4, length, width))
        self.one = jnp.concatenate(parts, 1)

    def far_line(self):
        self.arrived = lax.ppermute(self.one, BOTH, hop((8, 8)))
        return self.one

    def near_line(self, clock):
        self.arrived, clock = tie(self.arrived, clock)
        low = self.z < 2
        self.two = jnp.stack(
            [jnp.where(low, self.one, self.arrived), jnp.where(low, self.arrived, self.one)]
        )
        self.arrived = lax.ppermute(self.two, BOTH, hop((4, 4)))
        return self.two

    def plane(self, clock):
        self.arrived, clock = tie(self.arrived, clock)
        even = self.z % 2 == 0
        four = jnp.stack(
            [jnp.where(even, self.two, self.arrived), jnp.where(even, self.arrived, self.two)], 1
        )
        own = four.reshape(4, *self.one.shape)
        self.pieces = [own, lax.ppermute(own, BOTH, SECOND_HOP), lax.ppermute(own, BOTH, FIRST_HOP)]
        self.partner = [swap(own)]
        return own

    def corner(self, clock):
        self.pieces[1], clock = tie(self.pieces[1], clock)
        self.pieces.append(lax.ppermute(self.pieces[1], BOTH, FIRST_HOP))
        self.partner.append(swap(self.pieces[1]))
        return self.pieces[1]

    def pair(self, clock):
        self.pieces[2:], clock = tie(self.pieces[2:], clock)
        self.partner += [swap(piece) for piece in self.pieces[2:]]
        return self.pieces[3]

    def weights(self, after=()):
        place = lambda x, y: y * 2 + x
        here, across, corner = (
            place(self.x, self.y), place(1 - self.x, self.y), place(1 - self.x, 1 - self.y)
        )
        along = place(self.x, 1 - self.y)
        first = self.side == 0
        one, two = jnp.where(first, across, along), jnp.where(first, along, across)
        table = jnp.stack([self.side, here, one, two, corner, here, two, one, corner])
        outs = vmem_call(
            functools.partial(assemble_kernel, spots=self.spots),
            [jax.ShapeDtypeStruct(shape, BF16) for shape in self.shapes],
            table.astype(jnp.int32),
            *self.pieces,
            *self.partner,
            away=8,
            scratch_shapes=[pltpu.SemaphoreType.DMA(())],
            after=after,
        )
        return [out.reshape(-1, out.shape[3]) for out in outs]


class Bucket:
    def __init__(self, products, after=()):
        dp, side = lax.axis_index("dp"), lax.axis_index("band")
        self.x, self.y, self.z, self.side = dp % 2, dp // 2 % 2, dp // 4, side
        self.scalars = side[None].astype(jnp.int32)
        shapes, self.jobs, self.args = [], [], []
        for left, left_axis, right, right_axis in products:
            shapes.append((left.shape[1 - left_axis] // 16, right.shape[1 - right_axis] // 2))
            self.jobs.append((left_axis, right_axis))
            self.args += [left, right]
        self.spots, self.total = places(shapes)
        (self.send,) = vmem_call(
            functools.partial(send_kernel, jobs=self.jobs, spots=self.spots),
            [self.shaped(16)],
            self.scalars,
            *self.args,
            after=after,
        )

    def shaped(self, count):
        return jax.ShapeDtypeStruct((count, TILE, self.total), BF16)

    def block(self, index):
        return pl.BlockSpec((1, TILE, self.total), index)

    def split(self, count, table, goes, stays, after=()):
        goes, stays, out = self.block(goes), self.block(stays), self.block(lambda i, t: (i, 0, 0))
        self.send, self.keep = grid_call(
            split_kernel,
            table.astype(jnp.int32),
            (count,),
            [goes, stays, goes, stays],
            [out] * 2,
            [self.shaped(count)] * 2,
            self.keep,
            self.keep,
            self.arrived,
            self.arrived,
            after=after,
        )

    def pair_hop(self):
        self.arrived = swap(self.send)

    def first_hop(self, clock, after=()):
        self.arrived, clock = tie(self.arrived, clock)
        line = jnp.arange(8, dtype=jnp.int32)
        z, other = line // 2, line % 2
        near = jnp.where(self.side == 0, self.y, self.x)
        place = lambda bit: z * 4 + jnp.where(self.side == 0, bit * 2 + other, other * 2 + bit)
        table = jnp.concatenate([self.side[None], place(1 - near), place(near)])
        self.send, self.keep = vmem_call(
            functools.partial(keep_kernel, jobs=self.jobs, spots=self.spots),
            [self.shaped(8)] * 2,
            table.astype(jnp.int32),
            *self.args,
            self.arrived,
            away=1,
            scratch_shapes=[pltpu.VMEM((16, TILE, self.total), BF16), pltpu.SemaphoreType.DMA(())]
            + [pltpu.VMEM((16 * rows, half), F32) for rows, half, _ in self.spots],
            after=after,
        )
        self.arrived = lax.ppermute(self.send, BOTH, FIRST_HOP)
        return self.send

    def later_hop(self, clock, count, bit, pairs, after):
        self.arrived, clock = tie(self.arrived, clock)
        self.split(
            count,
            bit[None],
            lambda i, t: (2 * i + 1 - t[0], 0, 0),
            lambda i, t: (2 * i + t[0], 0, 0),
            after,
        )
        self.arrived = lax.ppermute(self.send, BOTH, pairs)
        return self.send

    def second_hop(self, clock, after=()):
        far = jnp.where(self.side == 0, self.x, self.y)
        return self.later_hop(clock, 4, far, SECOND_HOP, after)

    def third_hop(self, clock, after=()):
        return self.later_hop(clock, 2, self.z % 2, hop((4, 4)), after)

    def fourth_hop(self, clock, after=()):
        return self.later_hop(clock, 1, self.z // 2, hop((8, 8)), after)

    def finish(self):
        mine = (self.keep[0].astype(F32) + self.arrived[0].astype(F32)).astype(BF16)
        return vmem_call(
            functools.partial(unpack_kernel, spots=self.spots),
            [jax.ShapeDtypeStruct((r, 2 * h), F32) for r, h, _ in self.spots],
            self.scalars,
            mine,
            swap(mine),
        )


def tie(first, second):
    return lax.optimization_barrier((first, second))


def per_device(
    pixels, time_loc, band_mask, wavelengths, visible, band_table, cls_token, loc_weight,
    enc_attn_gain, enc_attn_shift, enc_qkv, enc_out, enc_mlp_gain, enc_mlp_shift, enc_up, enc_down,
    projection, mask_token, dec_attn_gain, dec_attn_shift, dec_qkv, dec_out, dec_mlp_gain,
    dec_mlp_shift, dec_up, dec_down, cotangent, *, device_count,
):
    side = lax.axis_index("band")
    table_rows = band_table.shape[0]
    wave_count, pixel_size = band_table.shape[1:]
    fast = device_count == 32
    enc_vectors = columns(
        [cls_token, enc_attn_gain, enc_attn_shift, enc_mlp_gain, enc_mlp_shift, loc_weight], 2 * LANES
    )
    dec_vectors = columns(
        [mask_token, dec_attn_gain, dec_attn_shift, dec_mlp_gain, dec_mlp_shift], 2 * LANES
    )
    shards = (
        [band_table.reshape(table_rows, -1), enc_vectors, enc_qkv, enc_out],
        [enc_up, enc_down, projection],
        [dec_vectors, dec_qkv, dec_out, dec_up, dec_down],
    )
    if fast:
        front, middle, back = (Gather(group, group[0].shape[0]) for group in shards)
        clock = front.far_line()
        clock = front.near_line(clock)
        middle.one, clock = tie(middle.one, clock)
        clock = middle.far_line()
        clock = front.plane(clock)
        clock = middle.near_line(clock)
        back.one, clock = tie(back.one, clock)
        clock = back.far_line()
        clock = front.corner(clock)
        clock = middle.plane(clock)
        clock = back.near_line(clock)
        clock = front.pair(clock)
        groups = [front.weights()]
    else:
        weights = gather_all([shard for group in shards for shard in group])
        groups = [weights[:4], weights[4:7], weights[7:]]
    table, enc_vectors, w_enc_qkv, w_enc_out = groups[0]
    enc_vec = enc_vectors.T.astype(F32)
    loc_rows = enc_vec[5 : 5 + loc_weight.shape[1]]

    def own_chip(array):
        mine = lax.dynamic_index_in_dim(array, side, 0, keepdims=False)
        theirs = lax.dynamic_index_in_dim(array, 1 - side, 0, keepdims=False)
        return jnp.concatenate([mine, swap(theirs)], -1)

    chip_pixels = own_chip(pixels)
    chip_mask, chip_waves = own_chip(jnp.stack([band_mask, wavelengths], 1))
    picks = visible[0]
    slot_wave = (chip_waves[:, None] == jnp.arange(wave_count, dtype=jnp.int32)) & (
        chip_mask[:, None] > 0
    )
    same_pixel = jnp.arange(pixel_size)[:, None] == jnp.arange(pixel_size)
    spread = (slot_wave[:, None, :, None] & same_pixel[None, :, None, :]).astype(BF16)
    spread = spread.reshape(chip_pixels.shape[1], wave_count * pixel_size)
    wave_pixels = jnp.pad(dot(chip_pixels, spread, 1, 0).astype(BF16), ((2, 0), (0, 0)))
    picks = jnp.pad(picks, (2, 0), constant_values=-1)
    band_count = jnp.sum(chip_mask).astype(F32)

    width = table.shape[0]
    patch_rows = dot(wave_pixels, table, 1, 1) / band_count + sincos(picks.astype(F32), width)
    loc_token = jnp.dot(time_loc, loc_rows, precision=lax.Precision.HIGHEST)
    tokens = jnp.concatenate([enc_vec[0:1], loc_token, patch_rows[2:]], 0)
    enc_half, enc_saved = attn_half(
        tokens, enc_vec[1], enc_vec[2], w_enc_qkv, w_enc_out, HEADS_ENC, HEADS_ENC
    )
    if fast:
        clock, enc_half = tie(clock, enc_half)
        clock = middle.corner(clock)
        clock = back.plane(clock)
        clock = middle.pair(clock)
        groups.append(middle.weights([enc_saved[5]]))
    w_enc_up, w_enc_down, w_proj = groups[1]
    enc_weights = (
        enc_vec[1], enc_vec[2], w_enc_qkv, w_enc_out, enc_vec[3], enc_vec[4], w_enc_up, w_enc_down
    )
    encoded, enc_saved = mlp_half(enc_half, enc_saved, *enc_weights[4:])
    latent_in = encoded.astype(BF16)
    latent = dot(latent_in, w_proj, 1, 0).astype(BF16)

    if fast:
        clock, latent = tie(clock, latent)
        clock = back.corner(clock)
        clock = back.pair(clock)
        groups.append(back.weights([latent]))
    dec_vectors, w_dec_qkv, w_dec_out, w_dec_up, w_dec_down = groups[2]
    dec_vec = dec_vectors.T.astype(F32)
    dec_weights = (
        dec_vec[1], dec_vec[2], w_dec_qkv, w_dec_out, dec_vec[3], dec_vec[4], w_dec_up, w_dec_down
    )
    positions = jnp.arange(cotangent.shape[1], dtype=jnp.int32)
    matches = positions[:, None] == picks[None, :]
    hidden = 1.0 - jnp.sum(matches.astype(F32), 1, keepdims=True)
    matches = matches.astype(BF16)
    inserted = (
        dot(matches, latent, 1, 0)
        + hidden * dec_vec[0]
        + sincos(positions.astype(F32), latent.shape[1])
    )
    dec_half, dec_saved = attn_half(inserted, *dec_weights[:4], HEADS_DEC, 8)
    decoded, dec_saved = mlp_half(dec_half, dec_saved, *dec_weights[4:])
    grad_out = cotangent[0].astype(F32)
    to_columns = jnp.eye(TILE, 2 * LANES, dtype=BF16)
    dec_branch, dec_upper, rest = mlp_backward(grad_out, dec_weights, dec_saved)
    grad_middle, dec_attn_branch, grad_attn, dec_norm_two = rest(dec_upper)
    dec_products = (
        (dec_saved[10], 0, dec_branch, 0),
        (dec_saved[8], 0, dec_upper, 0),
        (dec_saved[5], 1, dec_attn_branch, 0),
    )
    if fast:
        early = Bucket(dec_products)
        grad_attn, early.send = tie(grad_attn, early.send)
        early.pair_hop()
    dec_mixed = attn_backward(grad_attn, dec_saved, HEADS_DEC, 4)
    if fast:
        dec_mixed, early.send = tie(dec_mixed, early.first_hop(dec_mixed))
    dec_mixed = dec_mixed.reshape(dec_saved[3].shape)
    grad_inserted, dec_norm_one = input_backward(grad_middle, dec_mixed, dec_weights, dec_saved)
    grad_mask = jnp.sum(grad_inserted * hidden, 0)
    dec_vec_grads = vector_rows((grad_mask, *dec_norm_one, *dec_norm_two))
    grad_latent = dot(matches, grad_inserted.astype(BF16), 0, 0).astype(BF16)
    grad_encoded = dot(grad_latent, w_proj, 1, 1)

    enc_branch, enc_upper, rest = mlp_backward(grad_encoded, enc_weights, enc_saved)
    first_products = (
        (enc_saved[10], 0, enc_branch, 0),
        (enc_saved[8], 0, enc_upper, 0),
    )
    if fast:
        first = Bucket(first_products, [early.second_hop(enc_upper)])
        enc_upper, first.send = tie(enc_upper, first.send)
        first.pair_hop()
    grad_middle, enc_attn_branch, grad_attn, enc_norm_two = rest(enc_upper)
    enc_mixed = attn_backward(grad_attn, enc_saved, HEADS_ENC, HEADS_ENC)
    enc_mixed = enc_mixed.reshape(enc_saved[3].shape)
    second_products = (
        (enc_saved[5], 1, enc_attn_branch, 0),
        (enc_saved[2], 0, enc_mixed, 1),
        (dec_saved[2], 0, dec_mixed, 1),
        (latent_in, 0, grad_latent, 0),
        (dec_vec_grads, 0, to_columns, 0),
    )
    if fast:
        clock = first.first_hop(enc_mixed)
        enc_mixed, _ = tie(enc_mixed, early.third_hop(clock))
        second = Bucket(second_products)
        second.pair_hop()
        enc_mixed, _ = tie(enc_mixed, second.send)
    grad_tokens, enc_norm_one = input_backward(grad_middle, enc_mixed, enc_weights, enc_saved)
    grad_loc_row = grad_tokens[1:2]
    grad_time = jnp.dot(grad_loc_row, loc_rows.T, precision=lax.Precision.HIGHEST)
    grad_loc = time_loc[0][:, None] * grad_loc_row
    enc_vec_grads = vector_rows((grad_tokens[0], *enc_norm_one, *enc_norm_two, *grad_loc))
    grad_raw = (grad_tokens / band_count).astype(BF16)
    third_products = (
        (grad_raw, 0, wave_pixels, 0),
        (enc_vec_grads, 0, to_columns, 0),
    )
    if fast:
        third = Bucket(third_products)
        third.pair_hop()
        grad_raw, _ = tie(grad_raw, third.send)
    grad_waves = dot(grad_raw[2:], table, 1, 0).astype(BF16)
    grad_chip = dot(grad_waves, spread, 1, 1).astype(BF16)
    here = grad_chip.shape[1] // 2
    mine, theirs = grad_chip[:, :here], swap(grad_chip[:, here:])
    grad_pixels = jnp.where(
        side == 0, jnp.stack([mine, theirs]), jnp.stack([theirs, mine])
    ).astype(F32)
    if fast:
        clock = second.first_hop(grad_chip)
        clock = first.second_hop(clock, [clock])
        clock = third.first_hop(clock, [clock])
        clock = early.fourth_hop(clock, [clock])
        clock = first.third_hop(clock)
        clock = second.second_hop(clock)
        clock = third.second_hop(clock)
        early.arrived, clock = tie(early.arrived, clock)
        s_dec_down, s_dec_up, s_dec_out = early.finish()
        clock = first.fourth_hop(clock)
        clock = second.third_hop(clock)
        clock = third.third_hop(clock)
        clock = second.fourth_hop(clock)
        clock = third.fourth_hop(clock, [s_dec_up])
        s_enc_down, s_enc_up = first.finish()
        second_sums = second.finish()
        third_sums = third.finish()
    else:
        whole = lambda products: scatter_sums([
            dot(left, right, i, j).astype(BF16)
            for left, i, right, j in products
        ], device_count)
        s_dec_down, s_dec_up, s_dec_out = whole(dec_products)
        s_enc_down, s_enc_up = whole(first_products)
        second_sums, third_sums = whole(second_products), whole(third_products)
    s_enc_out, s_enc_qkv, s_dec_qkv, s_proj, s_dec_vec = second_sums
    s_table, s_enc_vec = third_sums
    return (
        decoded.astype(BF16)[None],
        grad_pixels,
        grad_time,
        s_table.reshape(band_table.shape),
        s_enc_vec[:, 0],
        s_enc_vec[:, 5 : 5 + loc_weight.shape[1]],
        s_enc_vec[:, 1],
        s_enc_vec[:, 2],
        s_enc_qkv,
        s_enc_out,
        s_enc_vec[:, 3],
        s_enc_vec[:, 4],
        s_enc_up,
        s_enc_down,
        s_proj,
        s_dec_vec[:, 0],
        s_dec_vec[:, 1],
        s_dec_vec[:, 2],
        s_dec_qkv,
        s_dec_out,
        s_dec_vec[:, 3],
        s_dec_vec[:, 4],
        s_dec_up,
        s_dec_down,
    )


def solution(mesh):
    dp, chip, both, matrix = P("dp"), P("dp", "band"), P(BOTH, None), P("dp", None)
    block = (dp, dp, matrix, matrix, dp, dp, matrix, matrix)
    in_specs = (
        P("dp", None, "band"), both, chip, chip, both,
        P("dp", None, None), dp, matrix, *block, matrix, dp, *block, P(BOTH, None, None),
    )
    out_specs = (
        P(BOTH, None, None), P("dp", None, "band"), both,
        P("dp", None, None), dp, matrix, *block, matrix, dp, *block,
    )
    return jax.shard_map(
        functools.partial(per_device, device_count=mesh.size),
        mesh=mesh, in_specs=in_specs, out_specs=out_specs, check_vma=False,
    )
```

```python
import functools
import math

import jax
import jax.numpy as jnp
from jax import lax
from jax.experimental import pallas as pl
from jax.experimental.pallas import tpu as pltpu
from jax.sharding import PartitionSpec as P

HEADS_ENC = 12
HEADS_DEC = 16
EPSILON = 1e-05
F32 = jnp.float32
BF16 = jnp.bfloat16
BOTH = ("dp", "band")


def dot(a, b, ca, cb):
    return lax.dot_general(a, b, (((ca,), (cb,)), ((), ())), preferred_element_type=F32)


def sincos(place_index, model_width):
    half_width = model_width // 2
    frequency = jnp.exp(-math.log(10000.0) * jnp.arange(half_width, dtype=F32) / half_width)
    angles = place_index[..., None] * frequency
    return jnp.concatenate([jnp.sin(angles), jnp.cos(angles)], -1)


def attend_forward_kernel(q_ref, k_ref, v_ref, out_ref, lse_ref, *, head_size, scale):
    log_scale = scale * math.log2(math.e)
    for first in range(0, q_ref.shape[0], head_size):
        rows = slice(first, first + head_size)
        scores = dot(k_ref[rows], q_ref[rows], 0, 0)
        top = jnp.max(scores, axis=0, keepdims=True) * log_scale
        weights = jnp.exp2(scores * log_scale - top)
        total = jnp.sum(weights, axis=0, keepdims=True)
        mixed = dot(v_ref[rows], weights.astype(BF16), 1, 0)
        out_ref[rows] = (mixed / total).astype(BF16)
        lse_ref[first // head_size] = top + jnp.log2(total)


def attend_forward(mixed_rows, head_count, heads_a_step):
    triple, length = mixed_rows.shape
    width = triple // 3
    head_size = width // head_count
    steps = head_count // heads_a_step
    slab = heads_a_step * head_size
    part = lambda which: pl.BlockSpec((slab, length), lambda h: (which * steps + h, 0))
    return pl.pallas_call(
        functools.partial(attend_forward_kernel, head_size=head_size, scale=head_size**-0.5),
        grid=(steps,),
        in_specs=[part(0), part(1), part(2)],
        out_specs=[part(0), pl.BlockSpec((heads_a_step, 1, length), lambda h: (h, 0, 0))],
        out_shape=[
            jax.ShapeDtypeStruct((width, length), BF16),
            jax.ShapeDtypeStruct((head_count, 1, length), F32),
        ],
        compiler_params=pltpu.CompilerParams(vmem_limit_bytes=40 << 20),
    )(mixed_rows, mixed_rows, mixed_rows)


def attend_backward_kernel(
    q_ref, k_ref, v_ref, out_ref, grad_ref, lse_ref, *rest, head_size, scale
):
    grad_mixed_ref = rest[-1]
    log_scale = scale * math.log2(math.e)
    for first in range(0, q_ref.shape[0], head_size):
        rows = slice(first, first + head_size)
        q, k, v, grad = q_ref[rows], k_ref[rows], v_ref[rows], grad_ref[rows]
        delta = jnp.sum(grad.astype(F32) * out_ref[rows].astype(F32), axis=0, keepdims=True)
        probs = jnp.exp2(dot(k, q, 0, 0) * log_scale - lse_ref[first // head_size])
        grad_probs = dot(v, grad, 0, 0)
        grad_scores = (probs * (grad_probs - delta)).astype(BF16)
        grad_mixed_ref[0, rows] = (dot(k, grad_scores, 1, 0) * scale).astype(BF16)
        grad_mixed_ref[1, rows] = (dot(q, grad_scores, 1, 1) * scale).astype(BF16)
        grad_mixed_ref[2, rows] = dot(grad, probs.astype(BF16), 1, 1).astype(BF16)


def attend_backward(
    mixed_rows, out_rows, grad_rows, lse, head_count, heads_a_step, share=(0, 1), before=None
):
    triple, length = mixed_rows.shape
    width = triple // 3
    head_size = width // head_count
    total = head_count // heads_a_step
    steps = total // share[1]
    start = share[0] * steps
    slab = heads_a_step * head_size
    part = lambda which: pl.BlockSpec((slab, length), lambda h: (which * total + start + h, 0))
    extra = [] if before is None else [before]
    return pl.pallas_call(
        functools.partial(attend_backward_kernel, head_size=head_size, scale=head_size**-0.5),
        grid=(steps,),
        in_specs=[
            part(0),
            part(1),
            part(2),
            part(0),
            part(0),
            pl.BlockSpec((heads_a_step, 1, length), lambda h: (start + h, 0, 0)),
        ]
        + [pl.BlockSpec(memory_space=pl.ANY) for _ in extra],
        out_specs=pl.BlockSpec((3, slab, length), lambda h: (0, start + h, 0)),
        out_shape=jax.ShapeDtypeStruct((3, width, length), BF16),
        input_output_aliases={6: 0} if extra else {},
        compiler_params=pltpu.CompilerParams(vmem_limit_bytes=40 << 20),
    )(mixed_rows, mixed_rows, mixed_rows, out_rows, grad_rows, lse, *extra)


def norm_forward(rows_in, gain_row, shift_row):
    centred = rows_in - jnp.mean(rows_in, -1, keepdims=True)
    inverse = lax.rsqrt(jnp.mean(centred * centred, -1, keepdims=True) + EPSILON)
    unit_rows = centred * inverse
    return (unit_rows * gain_row + shift_row).astype(BF16), unit_rows, inverse


def norm_backward(grad_normed, unit_rows, inverse, gain_row):
    grad_unit = grad_normed * gain_row
    grad_input = inverse * (
        grad_unit
        - jnp.mean(grad_unit, -1, keepdims=True)
        - unit_rows * jnp.mean(grad_unit * unit_rows, -1, keepdims=True)
    )
    return grad_input, jnp.sum(grad_normed * unit_rows, 0), jnp.sum(grad_normed, 0)


def gelu_tanh(upper):
    return jax.nn.gelu(upper, approximate=True)


def attn_half(rows_in, gain_one, shift_one, w_qkv, w_out, head_count, heads_a_step):
    normed_one, unit_one, inverse_one = norm_forward(rows_in, gain_one, shift_one)
    mixed_rows = dot(w_qkv, normed_one, 0, 1).astype(BF16)
    attn_rows, lse = attend_forward(mixed_rows, head_count, heads_a_step)
    middle = rows_in + dot(attn_rows, w_out, 0, 0)
    return middle, (unit_one, inverse_one, normed_one, mixed_rows, lse, attn_rows)


def mlp_half(middle, saved, gain_two, shift_two, w_up, w_down):
    normed_two, unit_two, inverse_two = norm_forward(middle, gain_two, shift_two)
    upper = dot(normed_two, w_up, 1, 0)
    active = gelu_tanh(upper).astype(BF16)
    rows_out = middle + dot(active, w_down, 1, 0)
    return rows_out, saved + (unit_two, inverse_two, normed_two, upper.astype(BF16), active)


def mlp_backward(grad_out, weights, saved):
    gain_two, w_out, w_up, w_down = weights[4], weights[3], weights[6], weights[7]
    unit_two, inverse_two, upper = saved[6], saved[7], saved[9]
    grad_branch = grad_out.astype(BF16)
    grad_active = dot(grad_branch, w_down, 1, 1)
    grad_upper = jax.vjp(gelu_tanh, upper.astype(F32))[1](grad_active)[0].astype(BF16)

    def rest(grad_upper):
        grad_normed = dot(grad_upper, w_up, 1, 1)
        grad_middle, grad_gain_two, grad_shift_two = norm_backward(
            grad_normed, unit_two, inverse_two, gain_two
        )
        grad_middle = grad_out + grad_middle
        grad_attn_branch = grad_middle.astype(BF16)
        grad_attn = dot(w_out, grad_attn_branch, 1, 1).astype(BF16)
        return grad_middle, grad_attn_branch, grad_attn, (grad_gain_two, grad_shift_two)

    return grad_branch, grad_upper, rest


def attn_backward(grad_attn, saved, head_count, heads_a_step, share=(0, 1), before=None):
    return attend_backward(
        saved[3], saved[5], grad_attn, saved[4], head_count, heads_a_step, share, before
    )


def input_backward(grad_middle, grad_mixed, weights, saved):
    grad_normed_one = dot(grad_mixed, weights[2], 0, 1)
    grad_input, grad_gain_one, grad_shift_one = norm_backward(
        grad_normed_one, saved[0], saved[1], weights[0]
    )
    return grad_middle + grad_input, (grad_gain_one, grad_shift_one)


def swap(array):
    return lax.ppermute(array, "band", [(0, 1), (1, 0)])


def join_pair(mine, axis):
    first = lax.axis_index("band") == 0
    other = swap(mine)
    return jnp.concatenate([jnp.where(first, mine, other), jnp.where(first, other, mine)], axis)


def groups_of(shards):
    rows = 0
    for shard in shards:
        rows = math.gcd(rows, shard.shape[0] // 2)
    return rows


def pack_rows(array, rows):
    lead, (length, width) = array.shape[:-2], array.shape[-2:]
    array = array.reshape(*lead, length // rows, rows, width)
    return jnp.swapaxes(array, -3, -2).reshape(*lead, rows, length // rows * width)


def unpack_rows(array, width):
    lead, (rows, total) = array.shape[:-2], array.shape[-2:]
    array = array.reshape(*lead, rows, total // width, width)
    return jnp.swapaxes(array, -3, -2).reshape(*lead, rows * (total // width), width)


def gather_all(shards):
    rows = groups_of(shards)
    side = lax.axis_index("band")
    halves = [
        lax.dynamic_slice_in_dim(s, side * (s.shape[0] // 2), s.shape[0] // 2, 0) for s in shards
    ]
    packed = jnp.concatenate([pack_rows(h, rows) for h in halves], 1)
    whole = lax.all_gather(packed, BOTH, axis=0, tiled=False)
    out, at = [], 0
    for half in halves:
        span = half.size // rows
        piece = unpack_rows(whole[:, :, at : at + span], half.shape[1])
        out.append(piece.reshape(-1, half.shape[1]))
        at += span
    return out


def pack_grads(grads, device_count):
    split = [g.reshape(device_count, -1, g.shape[1]) for g in grads]
    rows = 0
    for s in split:
        rows = math.gcd(rows, s.shape[1])
    return jnp.concatenate([pack_rows(s, rows) for s in split], 2)


def unpack_sums(summed, shapes):
    both = join_pair(summed[None], 0)
    rows = both.shape[1]
    out, at = [], 0
    for length, width in shapes:
        span = length // 2 * width // rows
        piece = unpack_rows(both[:, :, at : at + span], width)
        out.append(piece.reshape(length, width).astype(F32))
        at += span
    return out


def scatter_sums(grads, device_count):
    packed = pack_grads(grads, device_count)
    summed = lax.psum_scatter(packed, BOTH, scatter_dimension=0, tiled=False)
    dp_count = device_count // 2
    return unpack_sums(summed, [(g.shape[0] // dp_count, g.shape[1]) for g in grads])


LANES = 128
TILE = 16


def columns(vectors, lanes=LANES):
    stacked = jnp.concatenate([v if v.ndim == 2 else v[:, None] for v in vectors], 1)
    return jnp.pad(stacked, ((0, 0), (0, lanes - stacked.shape[1])))


def vector_rows(vectors):
    stacked = jnp.stack(vectors)
    return jnp.pad(stacked, ((0, TILE - stacked.shape[0]), (0, 0))).astype(BF16)


def hop(flips):
    return [
        (dp * 2 + band, (dp ^ flips[band]) * 2 + band) for dp in range(16) for band in range(2)
    ]


FIRST_HOP = hop((2, 1))
SECOND_HOP = hop((1, 2))


def places(shapes):
    out, at = [], 0
    for rows, half in shapes:
        out.append((rows, half, at))
        at += rows // TILE * half
    return out, at


def lay(dst, src, rows, half, at):
    for group in range(rows // TILE):
        dst[:, at + group * half : at + (group + 1) * half] = src[group * TILE : (group + 1) * TILE]


def products_of(jobs, spots, refs, which):
    ins = list(refs)
    for (left_axis, right_axis), spot in zip(jobs, spots):
        left, right = ins.pop(0), ins.pop(0)
        half = spot[1]
        span = pl.ds(pl.multiple_of(which * half, 128), half)
        values = right[span] if right_axis == 1 else right[:, span]
        yield dot(left[...], values, left_axis, right_axis)


def send_kernel(scalars, *refs, jobs, spots):
    out = refs[-1]
    halves = products_of(jobs, spots, refs[:-1], 1 - scalars[0])
    for values, (rows, half, at) in zip(halves, spots):
        values = values.astype(BF16)
        for block in range(16):
            lay(out.at[block], values[block * rows : (block + 1) * rows], rows, half, at)


def keep_kernel(scalars, *refs, jobs, spots):
    count = len(spots)
    arrived, send, keep, landed, sem = refs[-count - 5 : -count]
    copy = pltpu.make_async_copy(arrived, landed, sem)
    copy.start()
    halves = products_of(jobs, spots, refs[: -count - 5], scalars[0])
    for values, held in zip(halves, refs[-count:]):
        held[...] = values.astype(F32)
    copy.wait()
    for held, (rows, half, at) in zip(refs[-count:], spots):
        for step in range(16):
            block = scalars[1 + step]
            out = (send if step < 8 else keep).at[step % 8]
            for group in range(rows // TILE):
                span = slice(at + group * half, at + (group + 1) * half)
                own = held[pl.ds(pl.multiple_of(block * rows + group * TILE, TILE), TILE)]
                out[:, span] = (own + landed[block, :, span].astype(F32)).astype(BF16)


def split_kernel(table, own_send, own_keep, recv_send, recv_keep, send, keep):
    send[...] = (own_send[...].astype(F32) + recv_send[...].astype(F32)).astype(BF16)
    keep[...] = (own_keep[...].astype(F32) + recv_keep[...].astype(F32)).astype(BF16)


def unpack_kernel(scalars, mine, theirs, *outs, spots):
    side = scalars[0]
    for source, which in ((mine, side), (theirs, 1 - side)):
        for out, (rows, half, at) in zip(outs, spots):
            for group in range(rows // TILE):
                span = slice(at + group * half, at + (group + 1) * half)
                lanes = pl.ds(pl.multiple_of(which * half, 128), half)
                out[group * TILE : (group + 1) * TILE, lanes] = source[:, span].astype(F32)


def without(kernel, start, count):
    return lambda *refs: kernel(*refs[:start], *refs[start + count :])


def grid_call(kernel, scalars, grid, in_specs, out_specs, out_shape, *args, after=()):
    away = [pl.BlockSpec(memory_space=pl.ANY)] * len(after)
    return pl.pallas_call(
        without(kernel, 1 + len(args), len(after)),
        grid_spec=pltpu.PrefetchScalarGridSpec(
            num_scalar_prefetch=1, grid=grid, in_specs=in_specs + away, out_specs=out_specs
        ),
        out_shape=out_shape,
        compiler_params=pltpu.CompilerParams(vmem_limit_bytes=40 << 20),
    )(scalars, *args, *after)


def vmem_call(kernel, out_shape, *args, away=0, scratch_shapes=(), after=()):
    whole = pl.BlockSpec(memory_space=pltpu.VMEM)
    return pl.pallas_call(
        without(kernel, len(args), len(after)),
        in_specs=[pl.BlockSpec(memory_space=pltpu.SMEM)]
        + [whole] * (len(args) - 1 - away)
        + [pl.BlockSpec(memory_space=pl.ANY)] * (away + len(after)),
        out_specs=[whole] * len(out_shape),
        out_shape=out_shape,
        scratch_shapes=scratch_shapes,
        compiler_params=pltpu.CompilerParams(vmem_limit_bytes=56 << 20),
    )(*args, *after)


def assemble_kernel(scalars, *refs, spots):
    pieces, outs, sem = refs[:8], refs[8:-1], refs[-1]
    copies = []
    for index, piece in enumerate(pieces):
        line = scalars[1 + index]
        side = scalars[0] if index < 4 else 1 - scalars[0]
        for which, rows, first, half, at in spots:
            lanes = pl.ds(pl.multiple_of(side * half, 128), half)
            copies.append(
                pltpu.make_async_copy(
                    piece.at[:, :, at : at + half],
                    outs[which].at[:, line, first : first + rows, lanes],
                    sem,
                )
            )
    for copy in copies:
        copy.start()
    for copy in copies:
        copy.wait()


class Gather:
    def __init__(self, shards, rows):
        dp, side = lax.axis_index("dp"), lax.axis_index("band")
        self.x, self.y, self.z, self.side = dp % 2, dp // 2 % 2, dp // 4, side
        self.shapes, self.spots, parts, at = [], [], [], 0
        for which, shard in enumerate(shards):
            length, width = shard.shape
            half = width // 2
            mine = lax.dynamic_slice_in_dim(shard, side * half, half, 1)
            for first in range(0, length, rows):
                parts.append(mine[first : first + rows])
                self.spots.append((which, rows, first, half, at))
                at += half
            self.shapes.append((4, 4, length, width))
        self.one = jnp.concatenate(parts, 1)

    def far_line(self):
        self.arrived = lax.ppermute(self.one, BOTH, hop((8, 8)))
        return self.one

    def near_line(self, clock):
        self.arrived, clock = tie(self.arrived, clock)
        low = self.z < 2
        self.two = jnp.stack(
            [jnp.where(low, self.one, self.arrived), jnp.where(low, self.arrived, self.one)]
        )
        self.arrived = lax.ppermute(self.two, BOTH, hop((4, 4)))
        return self.two

    def plane(self, clock):
        self.arrived, clock = tie(self.arrived, clock)
        even = self.z % 2 == 0
        four = jnp.stack(
            [jnp.where(even, self.two, self.arrived), jnp.where(even, self.arrived, self.two)], 1
        )
        own = four.reshape(4, *self.one.shape)
        self.pieces = [own, lax.ppermute(own, BOTH, SECOND_HOP), lax.ppermute(own, BOTH, FIRST_HOP)]
        self.partner = [swap(own)]
        return own

    def corner(self, clock):
        self.pieces[1], clock = tie(self.pieces[1], clock)
        self.pieces.append(lax.ppermute(self.pieces[1], BOTH, FIRST_HOP))
        self.partner.append(swap(self.pieces[1]))
        return self.pieces[1]

    def pair(self, clock):
        self.pieces[2:], clock = tie(self.pieces[2:], clock)
        self.partner += [swap(piece) for piece in self.pieces[2:]]
        return self.pieces[3]

    def weights(self, after=()):
        place = lambda x, y: y * 2 + x
        here, across, corner = (
            place(self.x, self.y), place(1 - self.x, self.y), place(1 - self.x, 1 - self.y)
        )
        along = place(self.x, 1 - self.y)
        first = self.side == 0
        one, two = jnp.where(first, across, along), jnp.where(first, along, across)
        table = jnp.stack([self.side, here, one, two, corner, here, two, one, corner])
        outs = vmem_call(
            functools.partial(assemble_kernel, spots=self.spots),
            [jax.ShapeDtypeStruct(shape, BF16) for shape in self.shapes],
            table.astype(jnp.int32),
            *self.pieces,
            *self.partner,
            away=8,
            scratch_shapes=[pltpu.SemaphoreType.DMA(())],
            after=after,
        )
        return [out.reshape(-1, out.shape[3]) for out in outs]


class Bucket:
    def __init__(self, products, after=()):
        dp, side = lax.axis_index("dp"), lax.axis_index("band")
        self.x, self.y, self.z, self.side = dp % 2, dp // 2 % 2, dp // 4, side
        self.scalars = side[None].astype(jnp.int32)
        shapes, self.jobs, self.args = [], [], []
        for left, left_axis, right, right_axis in products:
            shapes.append((left.shape[1 - left_axis] // 16, right.shape[1 - right_axis] // 2))
            self.jobs.append((left_axis, right_axis))
            self.args += [left, right]
        self.spots, self.total = places(shapes)
        (self.send,) = vmem_call(
            functools.partial(send_kernel, jobs=self.jobs, spots=self.spots),
            [self.shaped(16)],
            self.scalars,
            *self.args,
            after=after,
        )

    def shaped(self, count):
        return jax.ShapeDtypeStruct((count, TILE, self.total), BF16)

    def block(self, index):
        return pl.BlockSpec((1, TILE, self.total), index)

    def split(self, count, table, goes, stays, after=()):
        goes, stays, out = self.block(goes), self.block(stays), self.block(lambda i, t: (i, 0, 0))
        self.send, self.keep = grid_call(
            split_kernel,
            table.astype(jnp.int32),
            (count,),
            [goes, stays, goes, stays],
            [out] * 2,
            [self.shaped(count)] * 2,
            self.keep,
            self.keep,
            self.arrived,
            self.arrived,
            after=after,
        )

    def pair_hop(self):
        self.arrived = swap(self.send)

    def first_hop(self, clock, after=()):
        self.arrived, clock = tie(self.arrived, clock)
        line = jnp.arange(8, dtype=jnp.int32)
        z, other = line // 2, line % 2
        near = jnp.where(self.side == 0, self.y, self.x)
        place = lambda bit: z * 4 + jnp.where(self.side == 0, bit * 2 + other, other * 2 + bit)
        table = jnp.concatenate([self.side[None], place(1 - near), place(near)])
        self.send, self.keep = vmem_call(
            functools.partial(keep_kernel, jobs=self.jobs, spots=self.spots),
            [self.shaped(8)] * 2,
            table.astype(jnp.int32),
            *self.args,
            self.arrived,
            away=1,
            scratch_shapes=[pltpu.VMEM((16, TILE, self.total), BF16), pltpu.SemaphoreType.DMA(())]
            + [pltpu.VMEM((16 * rows, half), F32) for rows, half, _ in self.spots],
            after=after,
        )
        self.arrived = lax.ppermute(self.send, BOTH, FIRST_HOP)
        return self.send

    def later_hop(self, clock, count, bit, pairs, after):
        self.arrived, clock = tie(self.arrived, clock)
        self.split(
            count,
            bit[None],
            lambda i, t: (2 * i + 1 - t[0], 0, 0),
            lambda i, t: (2 * i + t[0], 0, 0),
            after,
        )
        self.arrived = lax.ppermute(self.send, BOTH, pairs)
        return self.send

    def second_hop(self, clock, after=()):
        far = jnp.where(self.side == 0, self.x, self.y)
        return self.later_hop(clock, 4, far, SECOND_HOP, after)

    def third_hop(self, clock, after=()):
        return self.later_hop(clock, 2, self.z % 2, hop((4, 4)), after)

    def fourth_hop(self, clock, after=()):
        return self.later_hop(clock, 1, self.z // 2, hop((8, 8)), after)

    def finish(self):
        mine = (self.keep[0].astype(F32) + self.arrived[0].astype(F32)).astype(BF16)
        return vmem_call(
            functools.partial(unpack_kernel, spots=self.spots),
            [jax.ShapeDtypeStruct((r, 2 * h), F32) for r, h, _ in self.spots],
            self.scalars,
            mine,
            swap(mine),
        )


def tie(first, second):
    return lax.optimization_barrier((first, second))


def per_device(
    pixels, time_loc, band_mask, wavelengths, visible, band_table, cls_token, loc_weight,
    enc_attn_gain, enc_attn_shift, enc_qkv, enc_out, enc_mlp_gain, enc_mlp_shift, enc_up, enc_down,
    projection, mask_token, dec_attn_gain, dec_attn_shift, dec_qkv, dec_out, dec_mlp_gain,
    dec_mlp_shift, dec_up, dec_down, cotangent, *, device_count,
):
    side = lax.axis_index("band")
    table_rows = band_table.shape[0]
    wave_count, pixel_size = band_table.shape[1:]
    fast = device_count == 32
    enc_vectors = columns(
        [cls_token, enc_attn_gain, enc_attn_shift, enc_mlp_gain, enc_mlp_shift, loc_weight], 2 * LANES
    )
    dec_vectors = columns(
        [mask_token, dec_attn_gain, dec_attn_shift, dec_mlp_gain, dec_mlp_shift], 2 * LANES
    )
    shards = (
        [band_table.reshape(table_rows, -1), enc_vectors, enc_qkv, enc_out],
        [enc_up, enc_down, projection],
        [dec_vectors, dec_qkv, dec_out, dec_up, dec_down],
    )
    if fast:
        front, middle, back = (Gather(group, group[0].shape[0]) for group in shards)
        clock = front.far_line()
        clock = front.near_line(clock)
        middle.one, clock = tie(middle.one, clock)
        clock = middle.far_line()
        clock = front.plane(clock)
        clock = middle.near_line(clock)
        back.one, clock = tie(back.one, clock)
        clock = back.far_line()
        clock = front.corner(clock)
        clock = middle.plane(clock)
        clock = back.near_line(clock)
        clock = front.pair(clock)
        groups = [front.weights()]
    else:
        weights = gather_all([shard for group in shards for shard in group])
        groups = [weights[:4], weights[4:7], weights[7:]]
    table, enc_vectors, w_enc_qkv, w_enc_out = groups[0]
    enc_vec = enc_vectors.T.astype(F32)
    loc_rows = enc_vec[5 : 5 + loc_weight.shape[1]]

    def own_chip(array):
        mine = lax.dynamic_index_in_dim(array, side, 0, keepdims=False)
        theirs = lax.dynamic_index_in_dim(array, 1 - side, 0, keepdims=False)
        return jnp.concatenate([mine, swap(theirs)], -1)

    chip_pixels = own_chip(pixels)
    chip_mask, chip_waves = own_chip(jnp.stack([band_mask, wavelengths], 1))
    picks = visible[0]
    slot_wave = (chip_waves[:, None] == jnp.arange(wave_count, dtype=jnp.int32)) & (
        chip_mask[:, None] > 0
    )
    same_pixel = jnp.arange(pixel_size)[:, None] == jnp.arange(pixel_size)
    spread = (slot_wave[:, None, :, None] & same_pixel[None, :, None, :]).astype(BF16)
    spread = spread.reshape(chip_pixels.shape[1], wave_count * pixel_size)
    wave_pixels = jnp.pad(dot(chip_pixels, spread, 1, 0).astype(BF16), ((2, 0), (0, 0)))
    picks = jnp.pad(picks, (2, 0), constant_values=-1)
    band_count = jnp.sum(chip_mask).astype(F32)

    width = table.shape[0]
    patch_rows = dot(wave_pixels, table, 1, 1) / band_count + sincos(picks.astype(F32), width)
    loc_token = jnp.dot(time_loc, loc_rows, precision=lax.Precision.HIGHEST)
    tokens = jnp.concatenate([enc_vec[0:1], loc_token, patch_rows[2:]], 0)
    enc_half, enc_saved = attn_half(
        tokens, enc_vec[1], enc_vec[2], w_enc_qkv, w_enc_out, HEADS_ENC, HEADS_ENC
    )
    if fast:
        clock, enc_half = tie(clock, enc_half)
        clock = middle.corner(clock)
        clock = back.plane(clock)
        clock = middle.pair(clock)
        groups.append(middle.weights([enc_saved[5]]))
    w_enc_up, w_enc_down, w_proj = groups[1]
    enc_weights = (
        enc_vec[1], enc_vec[2], w_enc_qkv, w_enc_out, enc_vec[3], enc_vec[4], w_enc_up, w_enc_down
    )
    encoded, enc_saved = mlp_half(enc_half, enc_saved, *enc_weights[4:])
    latent_in = encoded.astype(BF16)
    latent = dot(latent_in, w_proj, 1, 0).astype(BF16)

    if fast:
        clock, latent = tie(clock, latent)
        clock = back.corner(clock)
        clock = back.pair(clock)
        groups.append(back.weights([latent]))
    dec_vectors, w_dec_qkv, w_dec_out, w_dec_up, w_dec_down = groups[2]
    dec_vec = dec_vectors.T.astype(F32)
    dec_weights = (
        dec_vec[1], dec_vec[2], w_dec_qkv, w_dec_out, dec_vec[3], dec_vec[4], w_dec_up, w_dec_down
    )
    positions = jnp.arange(cotangent.shape[1], dtype=jnp.int32)
    matches = positions[:, None] == picks[None, :]
    hidden = 1.0 - jnp.sum(matches.astype(F32), 1, keepdims=True)
    matches = matches.astype(BF16)
    inserted = (
        dot(matches, latent, 1, 0)
        + hidden * dec_vec[0]
        + sincos(positions.astype(F32), latent.shape[1])
    )
    dec_half, dec_saved = attn_half(inserted, *dec_weights[:4], HEADS_DEC, 8)
    decoded, dec_saved = mlp_half(dec_half, dec_saved, *dec_weights[4:])
    grad_out = cotangent[0].astype(F32)
    to_columns = jnp.eye(TILE, 2 * LANES, dtype=BF16)
    dec_branch, dec_upper, rest = mlp_backward(grad_out, dec_weights, dec_saved)
    grad_middle, dec_attn_branch, grad_attn, dec_norm_two = rest(dec_upper)
    dec_products = (
        (dec_saved[10], 0, dec_branch, 0),
        (dec_saved[8], 0, dec_upper, 0),
        (dec_saved[5], 1, dec_attn_branch, 0),
    )
    if fast:
        early = Bucket(dec_products)
        grad_attn, early.send = tie(grad_attn, early.send)
        early.pair_hop()
    dec_mixed = attn_backward(grad_attn, dec_saved, HEADS_DEC, 4)
    if fast:
        dec_mixed, early.send = tie(dec_mixed, early.first_hop(dec_mixed))
    dec_mixed = dec_mixed.reshape(dec_saved[3].shape)
    grad_inserted, dec_norm_one = input_backward(grad_middle, dec_mixed, dec_weights, dec_saved)
    grad_mask = jnp.sum(grad_inserted * hidden, 0)
    dec_vec_grads = vector_rows((grad_mask, *dec_norm_one, *dec_norm_two))
    grad_latent = dot(matches, grad_inserted.astype(BF16), 0, 0).astype(BF16)
    grad_encoded = dot(grad_latent, w_proj, 1, 1)

    enc_branch, enc_upper, rest = mlp_backward(grad_encoded, enc_weights, enc_saved)
    first_products = (
        (enc_saved[10], 0, enc_branch, 0),
        (enc_saved[8], 0, enc_upper, 0),
    )
    if fast:
        first = Bucket(first_products, [early.second_hop(enc_upper)])
        enc_upper, first.send = tie(enc_upper, first.send)
        first.pair_hop()
    grad_middle, enc_attn_branch, grad_attn, enc_norm_two = rest(enc_upper)
    enc_mixed = attn_backward(grad_attn, enc_saved, HEADS_ENC, HEADS_ENC)
    enc_mixed = enc_mixed.reshape(enc_saved[3].shape)
    second_products = (
        (enc_saved[5], 1, enc_attn_branch, 0),
        (enc_saved[2], 0, enc_mixed, 1),
        (dec_saved[2], 0, dec_mixed, 1),
        (latent_in, 0, grad_latent, 0),
        (dec_vec_grads, 0, to_columns, 0),
    )
    if fast:
        clock = first.first_hop(enc_mixed)
        enc_mixed, _ = tie(enc_mixed, early.third_hop(clock))
        second = Bucket(second_products)
        second.pair_hop()
        enc_mixed, _ = tie(enc_mixed, second.send)
    grad_tokens, enc_norm_one = input_backward(grad_middle, enc_mixed, enc_weights, enc_saved)
    grad_loc_row = grad_tokens[1:2]
    grad_time = jnp.dot(grad_loc_row, loc_rows.T, precision=lax.Precision.HIGHEST)
    grad_loc = time_loc[0][:, None] * grad_loc_row
    enc_vec_grads = vector_rows((grad_tokens[0], *enc_norm_one, *enc_norm_two, *grad_loc))
    grad_raw = (grad_tokens / band_count).astype(BF16)
    third_products = (
        (grad_raw, 0, wave_pixels, 0),
        (enc_vec_grads, 0, to_columns, 0),
    )
    if fast:
        third = Bucket(third_products)
        third.pair_hop()
        grad_raw, _ = tie(grad_raw, third.send)
    grad_waves = dot(grad_raw[2:], table, 1, 0).astype(BF16)
    grad_chip = dot(grad_waves, spread, 1, 1).astype(BF16)
    here = grad_chip.shape[1] // 2
    mine, theirs = grad_chip[:, :here], swap(grad_chip[:, here:])
    grad_pixels = jnp.where(
        side == 0, jnp.stack([mine, theirs]), jnp.stack([theirs, mine])
    ).astype(F32)
    if fast:
        clock = second.first_hop(grad_chip)
        clock = first.second_hop(clock, [clock])
        clock = third.first_hop(clock, [clock])
        clock = early.fourth_hop(clock, [clock])
        clock = first.third_hop(clock)
        clock = second.second_hop(clock)
        clock = third.second_hop(clock)
        early.arrived, clock = tie(early.arrived, clock)
        s_dec_down, s_dec_up, s_dec_out = early.finish()
        clock = first.fourth_hop(clock)
        clock = second.third_hop(clock)
        clock = third.third_hop(clock)
        clock = second.fourth_hop(clock)
        clock = third.fourth_hop(clock, [s_dec_up])
        s_enc_down, s_enc_up = first.finish()
        second_sums = second.finish()
        third_sums = third.finish()
    else:
        whole = lambda products: scatter_sums([
            dot(left, right, i, j).astype(BF16)
            for left, i, right, j in products
        ], device_count)
        s_dec_down, s_dec_up, s_dec_out = whole(dec_products)
        s_enc_down, s_enc_up = whole(first_products)
        second_sums, third_sums = whole(second_products), whole(third_products)
    s_enc_out, s_enc_qkv, s_dec_qkv, s_proj, s_dec_vec = second_sums
    s_table, s_enc_vec = third_sums
    return (
        decoded.astype(BF16)[None],
        grad_pixels,
        grad_time,
        s_table.reshape(band_table.shape),
        s_enc_vec[:, 0],
        s_enc_vec[:, 5 : 5 + loc_weight.shape[1]],
        s_enc_vec[:, 1],
        s_enc_vec[:, 2],
        s_enc_qkv,
        s_enc_out,
        s_enc_vec[:, 3],
        s_enc_vec[:, 4],
        s_enc_up,
        s_enc_down,
        s_proj,
        s_dec_vec[:, 0],
        s_dec_vec[:, 1],
        s_dec_vec[:, 2],
        s_dec_qkv,
        s_dec_out,
        s_dec_vec[:, 3],
        s_dec_vec[:, 4],
        s_dec_up,
        s_dec_down,
    )


def solution(mesh):
    dp, chip, both, matrix = P("dp"), P("dp", "band"), P(BOTH, None), P("dp", None)
    block = (dp, dp, matrix, matrix, dp, dp, matrix, matrix)
    in_specs = (
        P("dp", None, "band"), both, chip, chip, both,
        P("dp", None, None), dp, matrix, *block, matrix, dp, *block, P(BOTH, None, None),
    )
    out_specs = (
        P(BOTH, None, None), P("dp", None, "band"), both,
        P("dp", None, None), dp, matrix, *block, matrix, dp, *block,
    )
    return jax.shard_map(
        functools.partial(per_device, device_count=mesh.size),
        mesh=mesh, in_specs=in_specs, out_specs=out_specs, check_vma=False,
    )
```
